128 devices in a mesh: row: 8 (over z, core), col: 16 (over x, y).
Axes of the slice: x: 4, y: 4, z: 4, core: 2. Of those that a mesh axis runs over, the one named last changes fastest.
Arguments:
- start_block: float32 [32768, 128], P(('row', 'col')), may hold values from -6 to 6
- degree: float32 [32768], P(('row', 'col')), may hold values from 3.99 to 4.01
- block_values: float32 [49152, 4096], P(('row', 'col')), may hold values from -0.0007324219 to 0.0007324219
- block_rows: int32 [49152], P(('row', 'col')), may hold values from 0 to 31
- block_slots: int32 [49152], P(('row', 'col')), may hold values from 0 to 31, as said below
- need_lists: int32 [2048, 2], P(('row', 'col')), may hold values from 0 to 4, as said below
- live_blocks: int32 [128], P(('row', 'col')), may hold values from 96 to 384, as said below
Outputs:
- alphas: float32 [2, 128, 128], replicated
- betas: float32 [2, 128, 128], replicated
- next_basis: float32 [32768, 128], P(('row', 'col'))
The draws below stay inside these ranges and needn't reach their ends.
Inputs may be any that keep to these rules, and one draw needn't show every extreme that they name: `need_lists`: entries of a need list are distinct block rows, listed first, then padded with 4; every list has at least one entry, and on every device some list is full with 2 entries. `block_slots`: each slot's value p * 2 + q points at a listed (never padded) entry q of the device's need list p. `live_blocks`: some device uses all 384 slots in every draw.
All inputs are finite; a program needn't handle non-finite values.
Results may differ from the reference program's by a relative error of at most 0.00045.
Values sent between devices are 32-bit elements; how exact they have to be, the bound alone decides.
No kernel may reach another device: no remote copies, remote signals or barrier semaphores. Data moves between devices by JAX's collectives and lax.ppermute only.
A program may use at most 128 MiB of HBM per device.

```python
import jax
import jax.numpy as jnp
from jax import lax

BLK = 128
BS = 64
RB = 4
CAP = 384
ITERS = 2
KS = 2
NROWS = 32768
N_ROW = 8
N_COL = 16


def need_tables(key):
    devices_all = N_ROW * N_COL
    base_key = jax.random.fold_in(key, 7)
    key_order, key_count, key_full = jax.random.split(base_key, 3)
    scores = jax.random.randint(key_order, (devices_all, N_COL, RB), 0, 2 ** 20) * RB + jnp.arange(RB, dtype=jnp.int32)
    ordering = jnp.argsort(scores, axis=-1).astype(jnp.int32)
    counts = jax.random.randint(key_count, (devices_all, N_COL), 1, KS + 1)
    full_peer = jax.random.randint(key_full, (devices_all,), 0, N_COL)
    counts = jnp.where(jnp.arange(N_COL, dtype=jnp.int32)[None, :] == full_peer[:, None], KS, counts)
    positions = jnp.arange(KS, dtype=jnp.int32)
    lists = jnp.where(positions[None, None, :] < counts[:, :, None], ordering[:, :, :KS], RB)
    return (lists.astype(jnp.int32), counts.astype(jnp.int32))


def draw_need_lists(key, part):
    lists, counts = need_tables(key)
    return lists.reshape(N_ROW * N_COL * N_COL, KS)


def draw_block_slots(key, part):
    lists, counts = need_tables(key)
    devices_all = N_ROW * N_COL
    slot_key = jax.random.fold_in(key, 11)
    key_peer, key_pick = jax.random.split(slot_key)
    peers = jax.random.randint(key_peer, (devices_all, CAP), 0, N_COL)
    picks = jax.random.randint(key_pick, (devices_all, CAP), 0, 2 ** 16)
    peer_counts = jnp.take_along_axis(counts, peers, axis=1)
    slots = peers * KS + picks % peer_counts
    return slots.reshape(devices_all * CAP).astype(jnp.int32)


def draw_live_blocks(key, part):
    devices_all = N_ROW * N_COL
    live_key = jax.random.fold_in(key, 13)
    key_count, key_full = jax.random.split(live_key)
    counts = jax.random.randint(key_count, (devices_all,), CAP // 4, CAP + 1)
    full_device = jax.random.randint(key_full, (), 0, devices_all)
    counts = jnp.where(jnp.arange(devices_all, dtype=jnp.int32) == full_device, CAP, counts)
    return counts.astype(jnp.int32)


def draw_start_block(key, part):
    key = jax.random.fold_in(key, 17)
    key_noise, key_common = jax.random.split(key)
    noise = jax.random.normal(key_noise, (NROWS, BLK), jnp.float32)
    common = jax.random.normal(key_common, (NROWS, 1), jnp.float32)
    return jnp.clip(noise + 0.9 * common, -6.0, 6.0).astype(jnp.float32)


def place_ends(drawn, stream_key, smallest, top_value):
    shape = drawn.shape
    place = [jax.random.randint(jax.random.fold_in(stream_key, axis), (), 0, shape[axis]) for axis in range(len(shape))]
    drawn = drawn.at[tuple(place)].set(smallest)
    longest = shape.index(max(shape))
    place[longest] = (place[longest] + 1) % shape[longest]
    return drawn.at[tuple(place)].set(top_value)


def level_of(key, extent, cuts, low, high):
    def one(position, parts):
        steps = jax.random.uniform(jax.random.fold_in(jax.random.fold_in(key, 6), position), (parts,), jnp.float32, low / len(cuts), high / len(cuts))
        return jnp.repeat(jnp.exp(steps), extent[position] // parts).reshape((-1,) + (1,) * (len(extent) - position - 1))

    level = one(*cuts[0])
    for cut in cuts[1:]:
        level = level * one(*cut)
    return level


def gaussian(key, shape, scale, limit, shards=(), kind=jnp.bfloat16):
    values = jax.random.normal(key, shape, jnp.float32) * scale
    if len(shards) > 0:
        values = level_of(key, shape, shards, -0.22, 0.18) * values
    return jnp.clip(values, min=-limit, max=limit).astype(kind)


def setup_inputs(seed: int = 0) -> dict:
    key_of = jax.random.split(jax.random.key(seed), 8)
    start_block = draw_start_block(jax.random.fold_in(key_of[7], 71), 0)
    degree = jnp.clip(3.99 + 0.02000022 * jax.random.uniform(key_of[1], (NROWS,), jnp.float32) ** level_of(key_of[1], (NROWS,), ((0, 128),), -0.2, 0.2), 3.99, 4.01)
    block_values = gaussian(key_of[2], (N_ROW * N_COL * CAP, BS * BS), (4096 * 3 * CAP * BS // RB) ** -0.5, 0.0007324219, ((0, 128),), jnp.float32)
    block_rows = place_ends(jax.random.randint(key_of[3], (N_ROW * N_COL * CAP,), 0, N_ROW * RB), jax.random.fold_in(key_of[3], 1), 0, (N_ROW * RB) - 1).astype(jnp.int32)
    block_slots = draw_block_slots(jax.random.fold_in(key_of[7], 71), 0)
    need_lists = draw_need_lists(jax.random.fold_in(key_of[7], 71), 0)
    live_blocks = draw_live_blocks(jax.random.fold_in(key_of[7], 71), 0)
    return {"start_block": start_block, "degree": degree, "block_values": block_values, "block_rows": block_rows, "block_slots": block_slots, "need_lists": need_lists, "live_blocks": live_blocks}


HIGH = lax.Precision.HIGHEST

def gram_of(left, right):
    return jnp.einsum('ra,rb->ab', left, right, precision=HIGH) / NROWS

def next_block(image_block):
    lower_factor = jnp.linalg.cholesky(gram_of(image_block, image_block))
    solved = lax.linalg.triangular_solve(lower_factor, image_block, left_side=False, lower=True, transpose_a=True)
    return (solved, lower_factor.T)

def apply_matrix(current, degree, block_values, block_rows, block_slots, need_lists, live_blocks):
    devices_all = N_ROW * N_COL
    vector_grid = current.reshape(N_ROW, N_COL, RB, BS, BLK)
    values_all = block_values.reshape(devices_all, CAP, BS, BS)
    rows_all = block_rows.reshape(devices_all, CAP)
    slots_all = block_slots.reshape(devices_all, CAP)
    needs_all = need_lists.reshape(devices_all, N_COL * KS)

    def device_step(total, inputs):
        device_id, values_now, rows_now, slots_now, needs_now, count_now = inputs
        row_position = device_id // N_COL
        col_position = device_id % N_COL
        in_use = (jnp.arange(CAP, dtype=jnp.int32) < count_now).astype(current.dtype)
        blocks_now = values_now * in_use[:, None, None]
        cols_now = slots_now // KS * RB + needs_now[slots_now]
        col_side = lax.dynamic_index_in_dim(vector_grid, row_position, 0, False).reshape(N_COL * RB, BS, BLK)
        row_side = lax.dynamic_index_in_dim(vector_grid, col_position, 1, False).reshape(N_ROW * RB, BS, BLK)
        forward = jnp.einsum('sab,sbn->san', blocks_now, col_side[cols_now], precision=HIGH)
        backward = jnp.einsum('sba,sbn->san', blocks_now, row_side[rows_now], precision=HIGH)
        row_part = jnp.zeros((N_ROW * RB, BS, BLK), current.dtype).at[rows_now].add(forward)
        col_part = jnp.zeros((N_COL * RB, BS, BLK), current.dtype).at[cols_now].add(backward)
        total = total.at[:, col_position].add(row_part.reshape(N_ROW, RB, BS, BLK))
        total = total.at[row_position].add(col_part.reshape(N_COL, RB, BS, BLK))
        return (total, None)
    start_total = jnp.zeros((N_ROW, N_COL, RB, BS, BLK), current.dtype)
    device_ids = jnp.arange(devices_all, dtype=jnp.int32)
    total, _ = lax.scan(device_step, start_total, (device_ids, values_all, rows_all, slots_all, needs_all, live_blocks))
    return degree[:, None] * current - total.reshape(NROWS, BLK)

def reference(start_block, degree, block_values, block_rows, block_slots, need_lists, live_blocks):
    lower_factor = jnp.linalg.cholesky(gram_of(start_block, start_block))
    current = lax.linalg.triangular_solve(lower_factor, start_block, left_side=False, lower=True, transpose_a=True)
    basis_list = [current]
    alpha_list = []
    beta_list = []
    for iteration in range(ITERS):
        image_block = apply_matrix(current, degree, block_values, block_rows, block_slots, need_lists, live_blocks)
        alpha_block = gram_of(current, image_block)
        image_block = image_block - jnp.dot(current, alpha_block, precision=HIGH)
        if iteration > 0:
            image_block = image_block - jnp.dot(basis_list[-2], beta_list[-1].T, precision=HIGH)
        stacked = jnp.concatenate(basis_list, axis=1)
        image_block = image_block - jnp.dot(stacked, gram_of(stacked, image_block), precision=HIGH)
        current, beta_block = next_block(image_block)
        alpha_list.append(alpha_block)
        beta_list.append(beta_block)
        basis_list.append(current)
    return (jnp.stack(alpha_list), jnp.stack(beta_list), current)
```

```python
import functools

import jax
import jax.numpy as jnp
from jax import lax
from jax.experimental import pallas as pl
from jax.experimental.pallas import tpu as pltpu
from jax.sharding import PartitionSpec as P

BS = 64
RB = 4
KS = 2
NB = 128
ROWS = RB * BS
N_ROW = 8
N_COL = 16
NROWS = ROWS * N_ROW * N_COL
CAP = 384
SIDE = 2048
SHIFT = 4.0
GROUPS = CAP // 8
STEP_GROUPS = 6
FILL_STEPS = GROUPS // STEP_GROUPS
CHUNK = 256
CHUNKS = SIDE // CHUNK
SUMS = 24

HIGH = lax.Precision.HIGHEST
F32, BF16 = jnp.float32, jnp.bfloat16
MIB = 2**20


def mm(a, b, ca=1, cb=0):
    return lax.dot_general(a, b, (((ca,), (cb,)), ((), ())), precision=HIGH, preferred_element_type=F32)


def split(x):
    high = x.astype(BF16)
    return high, (x - high.astype(F32)).astype(BF16)


def dense_kernel(rows_ref, slots_ref, live_ref, vals_ref, hi_ref, lo_ref, dense):
    i = pl.program_id(0)
    live = live_ref[0]

    @pl.when(i == 0)
    def _():
        def clear(t, c):
            dense[t // 8, pl.ds(pl.multiple_of((t % 8) * 256, 256), 256), :] = jnp.zeros((256, 128), F32)
            return c

        lax.fori_loop(0, 128, clear, 0)

    half = lax.broadcasted_iota(jnp.int32, (32, 128), 1) // 64

    @pl.when(i < FILL_STEPS)
    def _():
        def group(g, c):
            for s in range(8):
                slot = (i * STEP_GROUPS + g) * 8 + s
                first = rows_ref[slot] * BS
                q = slots_ref[slot]
                side = jnp.where(slot < live, q % 2, 2)
                two = vals_ref[g, pl.ds(s, 32, stride=8), :]
                turned = pltpu.roll(two, 64, 1)
                even = jnp.where(half == side, jnp.where(half == 0, two, turned), 0.0)
                odd = jnp.where(half == side, jnp.where(half == 0, turned, two), 0.0)
                dense[q // 2, pl.ds(first, 32, stride=2), :] += even
                dense[q // 2, pl.ds(first + 1, 32, stride=2), :] += odd
            return c

        left = (live + 7) // 8 - i * STEP_GROUPS
        lax.fori_loop(0, jnp.clip(left, 0, STEP_GROUPS), group, 0)

    @pl.when(i >= FILL_STEPS)
    def _():
        first = pl.multiple_of((i - FILL_STEPS) * CHUNK, CHUNK)
        for j in range(16):
            high, low = split(dense[j, pl.ds(first, CHUNK), :])
            hi_ref[:, j * 128 : (j + 1) * 128] = high
            lo_ref[:, j * 128 : (j + 1) * 128] = low


def dense_of(values, rel_rows, slots, live):
    grid = FILL_STEPS + CHUNKS
    out = pl.BlockSpec((CHUNK, SIDE), lambda i, *_: (jnp.maximum(i - FILL_STEPS, 0), 0))
    return pl.pallas_call(
        dense_kernel,
        grid_spec=pltpu.PrefetchScalarGridSpec(
            num_scalar_prefetch=3,
            grid=(grid,),
            in_specs=[pl.BlockSpec((STEP_GROUPS, 256, 128), lambda i, *_: (jnp.minimum(i, FILL_STEPS - 1), 0, 0))],
            out_specs=[out, out],
            scratch_shapes=[pltpu.VMEM((16, SIDE, 128), F32)],
        ),
        out_shape=[jax.ShapeDtypeStruct((SIDE, SIDE), BF16)] * 2,
        compiler_params=pltpu.CompilerParams(vmem_limit_bytes=40 * MIB),
        cost_estimate=pl.CostEstimate(flops=10**7, bytes_accessed=50 * 10**6, transcendentals=0),
        name="dense",
    )(rel_rows, slots, live, values)


def product_kernel(whole, need_ref, hi_ref, lo_ref, own, z1, z2, z3, far, cols, extra, keep, send, pay, xc, xr, acc):
    i = pl.program_id(0)

    @pl.when(i == 0)
    def _():
        def column(p, c):
            for k in range(KS):
                if whole:
                    first = jnp.minimum(need_ref[p * KS + k], RB - 1) * BS
                    block = cols[p, pl.ds(pl.multiple_of(first, BS), BS), :]
                else:
                    block = cols[p, k * BS : (k + 1) * BS, :]
                high, low = split(block)
                here = pl.ds(pl.multiple_of((p * KS + k) * BS, BS), BS)
                xc[here, 0:128] = high
                xc[here, 128:256] = low
            return c

        lax.fori_loop(0, N_COL, column, 0)
        for c in range(CHUNKS):
            piece = (own, z1, z2, z3)[c][...] if c < 4 else far[(c - 4) * CHUNK : (c - 3) * CHUNK, :]
            high, low = split(piece.T)
            xr[c, 0:128, :] = high
            xr[c, 128:256, :] = low

    hi, lo, x = hi_ref[...], lo_ref[...], xc[...]
    out = jnp.dot(hi, x, preferred_element_type=F32) + jnp.dot(lo, x, preferred_element_type=F32)
    out = out[:, :128] + out[:, 128:]

    @pl.when(i < 4)
    def _():
        keep[jnp.minimum(i, 3)] = out

    @pl.when(i >= 4)
    def _():
        send[jnp.maximum(i - 4, 0)] = out

    v = xr[i]
    for j in range(4):
        here = slice(j * 512, (j + 1) * 512)
        part = jnp.dot(v, hi_ref[:, here], preferred_element_type=F32) + jnp.dot(
            v, lo_ref[:, here], preferred_element_type=F32
        )
        before = acc[:, here]
        acc[:, here] = jnp.where(i == 0, part, before + part)

    @pl.when(i == CHUNKS - 1)
    def _():
        for p in range(N_COL):
            here = slice(p * 128, (p + 1) * 128)
            pay[p, 0:128, :] = (acc[0:128, here] + acc[128:256, here]).T
            pay[p, 128:, :] = extra[p]


def products(whole, need, hi, lo, pieces, cols, extra):
    def full(shape):
        return pl.BlockSpec(shape, lambda i, *_: (0,) * len(shape))

    more = extra.shape[1]
    chunk = pl.BlockSpec((CHUNK, SIDE), lambda i, *_: (i, 0))
    return pl.pallas_call(
        functools.partial(product_kernel, whole),
        grid_spec=pltpu.PrefetchScalarGridSpec(
            num_scalar_prefetch=1,
            grid=(CHUNKS,),
            in_specs=[chunk, chunk] + [full((ROWS, NB))] * 4 + [full((4 * ROWS, NB)), full(cols.shape), full(extra.shape)],
            out_specs=[full((4, ROWS, NB)), full((4, ROWS, NB)), full((N_COL, 128 + more, NB))],
            scratch_shapes=[
                pltpu.VMEM((SIDE, 256), BF16),
                pltpu.VMEM((CHUNKS, 256, CHUNK), BF16),
                pltpu.VMEM((256, SIDE), F32),
            ],
        ),
        out_shape=[
            jax.ShapeDtypeStruct((4, ROWS, NB), F32),
            jax.ShapeDtypeStruct((4, ROWS, NB), F32),
            jax.ShapeDtypeStruct((N_COL, 128 + more, NB), F32),
        ],
        compiler_params=pltpu.CompilerParams(vmem_limit_bytes=40 * MIB),
        cost_estimate=pl.CostEstimate(flops=8 * 10**9, bytes_accessed=22 * 10**6, transcendentals=0),
        name="products",
    )(need, hi, lo, *pieces, cols, extra)


def image_of(v, deg, s0, s1, s2, s3, arrived, needs):
    sums = s0[...] + s1[...] + s2[...] + s3[...]

    def peer(p, parts):
        for q in range(KS):
            block = arrived[p, q * BS : (q + 1) * BS, :]
            which = needs[p, q : q + 1, :]
            parts = tuple(parts[k] + jnp.where(which == float(k), block, 0.0) for k in range(RB))
        return parts

    zero = jnp.zeros((BS, NB), F32)
    parts = lax.fori_loop(0, N_COL, peer, (zero,) * RB)
    return (deg[...] - SHIFT) * v[...] - sums - jnp.concatenate(parts, axis=0)


def first_kernel(v, deg, s0, s1, s2, s3, arrived, image, pay, needs):
    needs[...] = arrived[:, 128:136, :]
    y = image_of(v, deg, s0, s1, s2, s3, arrived, needs)
    image[...] = y
    for p in range(N_COL):
        for q in range(KS):
            which = needs[p, q : q + 1, :]
            block = jnp.zeros((BS, NB), F32)
            for k in range(RB):
                block = jnp.where(which == float(k), image[k * BS : (k + 1) * BS, :], block)
            pay[p, q * BS : (q + 1) * BS, :] = block
    x = v[...]
    xt, yt = x.T, y.T
    for at, gram in ((128, mm(xt, x)), (136, mm(xt, y)), (144, mm(yt, y))):
        gram = gram * (1.0 / NROWS)
        for p in range(N_COL):
            pay[p, at : at + 8, :] = gram[8 * p : 8 * p + 8, :]


def first_image(v, deg, sums, arrived):
    return pl.pallas_call(
        first_kernel,
        out_shape=[
            jax.ShapeDtypeStruct((ROWS, NB), F32),
            jax.ShapeDtypeStruct((N_COL, 128 + SUMS, NB), F32),
            jax.ShapeDtypeStruct((N_COL, 8, NB), F32),
        ],
        compiler_params=pltpu.CompilerParams(vmem_limit_bytes=32 * MIB),
        name="first_image",
    )(v, deg, *sums, arrived)


PANEL = 16


def factor(a):
    lane = lax.broadcasted_iota(jnp.int32, (NB, NB), 1)
    sub = lax.broadcasted_iota(jnp.int32, (NB, NB), 0)
    z = jnp.where(lane == sub, 1.0, 0.0)
    row = lax.broadcasted_iota(jnp.int32, (PANEL, NB), 0)
    uppers, inverses = [], []
    for b in range(NB // PANEL):
        pa, pz = a[:PANEL], z[:PANEL]
        for t in range(PANEL):
            k = b * PANEL + t
            scale = lax.rsqrt(pa[t : t + 1, k : k + 1])
            ra, rz = pa[t : t + 1] * scale, pz[t : t + 1] * scale
            times = pa[:, k : k + 1] * scale
            pa = jnp.where(row == t, ra, jnp.where(row > t, pa - times * ra, pa))
            pz = jnp.where(row == t, rz, jnp.where(row > t, pz - times * rz, pz))
        uppers.append(pa)
        inverses.append(pz)
        if b < NB // PANEL - 1:
            done = (b + 1) * PANEL
            left = pa.T[done:, :]
            a = a[PANEL:] - mm(left, pa)
            z = z[PANEL:] - mm(left, pz)
    upper = jnp.where(lane >= sub, jnp.concatenate(uppers, axis=0), 0.0)
    return upper, jnp.concatenate(inverses, axis=0)


def eye():
    return jnp.where(
        lax.broadcasted_iota(jnp.int32, (NB, NB), 0) == lax.broadcasted_iota(jnp.int32, (NB, NB), 1), 1.0, 0.0
    )


def second_kernel(x_ref, y_ref, deg, s0, s1, s2, s3, arrived, needs, alpha, beta, v0_ref, v1_ref, w_ref, gram):
    y2 = image_of(y_ref, deg, s0, s1, s2, s3, arrived, needs)
    xx, xy, yy = (
        jnp.concatenate([arrived[p, at : at + 8, :] for p in range(N_COL)], axis=0) for at in (128, 136, 144)
    )
    x, y = x_ref[...], y_ref[...]
    _, inv0 = factor(xx)
    a0 = mm(mm(inv0, xy), inv0, 1, 1)
    b0 = mm(mm(inv0, yy), inv0, 1, 1)
    alpha[...] = a0 + SHIFT * eye()
    upper1, inv1 = factor(b0 - mm(a0, a0, 0, 0))
    beta[...] = upper1
    v0 = mm(x, inv0, 1, 1)
    t = mm(inv0, inv1, 0, 1)
    u = mm(mm(inv0, a0, 0, 0), inv1, 1, 1)
    v1 = mm(y, t) - mm(x, u)
    w = mm(y2, t) - mm(y, u)
    v0_ref[...], v1_ref[...], w_ref[...] = v0, v1, w
    gram[0:128, :] = mm(v0.T, w) * (1.0 / NROWS)
    gram[128:256, :] = mm(v1.T, w) * (1.0 / NROWS)
    gram[256:384, :] = mm(w.T, w) * (1.0 / NROWS)


def second_image(x, y, deg, sums, arrived, needs):
    square = jax.ShapeDtypeStruct((NB, NB), F32)
    owned = jax.ShapeDtypeStruct((ROWS, NB), F32)
    return pl.pallas_call(
        second_kernel,
        out_shape=[square, square, owned, owned, owned, jax.ShapeDtypeStruct((3 * NB, NB), F32)],
        compiler_params=pltpu.CompilerParams(vmem_limit_bytes=32 * MIB),
        name="second_image",
    )(x, y, deg, *sums, arrived, needs)


def last_kernel(v0, v1, w, gram, alpha0, beta0, alphas, betas, basis):
    a0, a1, b = gram[0:128, :], gram[128:256, :], gram[256:384, :]
    upper, inv = factor(b - mm(a0, a0, 0, 0) - mm(a1, a1, 0, 0))
    alphas[0], betas[0] = alpha0[...], beta0[...]
    alphas[1] = a1 + SHIFT * eye()
    betas[1] = upper
    w2 = w[...] - mm(v0[...], a0) - mm(v1[...], a1)
    basis[...] = mm(w2, inv, 1, 1)


def last_block(*args):
    pair = jax.ShapeDtypeStruct((2, NB, NB), F32)
    return pl.pallas_call(
        last_kernel,
        out_shape=[pair, pair, jax.ShapeDtypeStruct((ROWS, NB), F32)],
        compiler_params=pltpu.CompilerParams(vmem_limit_bytes=32 * MIB),
        name="last_block",
    )(*args)


CORE = [(i, i ^ 1) for i in range(N_ROW)]


def along_z(k):
    return [(i, ((i // 2 + k) % 4) * 2 + i % 2) for i in range(N_ROW)]


def along_x(k):
    return [(i, ((i // 4 + k) % 4) * 4 + i % 4) for i in range(N_COL)]


def along_y(k):
    return [(i, (i // 4) * 4 + (i % 4 + k) % 4) for i in range(N_COL)]


def row_pieces(own):
    three = [lax.ppermute(own, "row", along_z(k)) for k in (3, 2, 1)]
    far = lax.ppermute(jnp.concatenate([own, *three]), "row", CORE)
    return [own, *three, far]


def row_sums(keep, send):
    other = lax.ppermute(send, "row", CORE)
    parts = [keep[k] + other[k] for k in range(4)]
    return [parts[0]] + [lax.ppermute(parts[k], "row", along_z(k)) for k in (1, 2, 3)]


def swap(x):
    return lax.all_to_all(x, "col", 0, 0)


def ring_sum(x, axis, shift):
    return x + sum(lax.ppermute(x, axis, shift(k)) for k in (1, 3, 2))


def sum_all(x):
    core = lax.axis_index("row") % 2
    n = x.shape[0] // 2
    here = jnp.where(core == 0, x[:n], x[n:])
    there = jnp.where(core == 0, x[n:], x[:n])
    here = here + lax.ppermute(there, "row", CORE)
    here = ring_sum(here, "row", along_z)
    here = ring_sum(here, "col", along_x)
    here = ring_sum(here, "col", along_y)
    other = lax.ppermute(here, "row", CORE)
    return jnp.concatenate([jnp.where(core == 0, here, other), jnp.where(core == 0, other, here)])


def on_device(start_block, degree, block_values, block_rows, block_slots, need_lists, live_blocks):
    row = lax.axis_index("row")
    z, core = row // 2, row % 2
    owner, k = block_rows // RB, block_rows % RB
    rel_rows = (((owner % 2) ^ core) * 4 + (owner // 2 - z) % 4) * RB + k
    need = need_lists.reshape(-1)
    needs_out = jnp.broadcast_to(
        jnp.pad(need_lists.astype(F32), ((0, 0), (0, 8 - KS)))[:, :, None], (N_COL, 8, NB)
    )
    deg = jnp.broadcast_to(degree[:, None], (ROWS, NB))
    values = block_values.reshape(GROUPS, 8, 32, 128).transpose(0, 2, 1, 3).reshape(GROUPS, 256, 128)

    cols = swap(jnp.broadcast_to(start_block[None], (N_COL, ROWS, NB)))
    pieces = row_pieces(start_block)
    hi, lo = dense_of(values, rel_rows, block_slots, live_blocks)
    keep, send, pay = products(True, need, hi, lo, pieces, cols, needs_out)
    sums = row_sums(keep, send)
    y, pay, needs = first_image(start_block, deg, sums, swap(pay))

    cols = swap(pay)
    pieces = row_pieces(y)
    part = cols[:, 128:, :].sum(0)
    part = part + lax.ppermute(part, "row", CORE)
    part = ring_sum(part, "row", along_z)
    zero = jnp.zeros((N_COL, SUMS, NB), F32)
    keep, send, pay = products(False, need, hi, lo, pieces, cols, zero)
    pay = pay.at[:, 128:, :].set(jnp.broadcast_to(part[None], (N_COL, SUMS, NB)))
    sums = row_sums(keep, send)
    alpha, beta, v0, v1, w, gram = second_image(start_block, y, deg, sums, swap(pay), needs)
    return tuple(last_block(v0, v1, w, sum_all(gram), alpha, beta))


def solution(mesh):
    return jax.shard_map(
        on_device,
        mesh=mesh,
        in_specs=(
            P(("row", "col"), None),
            P(("row", "col")),
            P(("row", "col"), None),
            P(("row", "col")),
            P(("row", "col")),
            P(("row", "col"), None),
            P(("row", "col")),
        ),
        out_specs=(P(), P(), P(("row", "col"), None)),
        check_vma=False,
    )
```

```python
import functools

import jax
import jax.numpy as jnp
from jax import lax
from jax.experimental import pallas as pl
from jax.experimental.pallas import tpu as pltpu
from jax.sharding import PartitionSpec as P

BS = 64
RB = 4
KS = 2
NB = 128
ROWS = RB * BS
N_ROW = 8
N_COL = 16
NROWS = ROWS * N_ROW * N_COL
CAP = 384
SIDE = 2048
SHIFT = 4.0
GROUPS = CAP // 8
STEP_GROUPS = 6
FILL_STEPS = GROUPS // STEP_GROUPS
CHUNK = 256
CHUNKS = SIDE // CHUNK
SUMS = 24

HIGH = lax.Precision.HIGHEST
F32, BF16 = jnp.float32, jnp.bfloat16
MIB = 2**20


def mm(a, b, ca=1, cb=0):
    return lax.dot_general(a, b, (((ca,), (cb,)), ((), ())), precision=HIGH, preferred_element_type=F32)


def split(x):
    high = x.astype(BF16)
    return high, (x - high.astype(F32)).astype(BF16)


def dense_kernel(rows_ref, slots_ref, live_ref, vals_ref, hi_ref, lo_ref, dense):
    i = pl.program_id(0)
    live = live_ref[0]

    @pl.when(i == 0)
    def _():
        def clear(t, c):
            dense[t // 8, pl.ds(pl.multiple_of((t % 8) * 256, 256), 256), :] = jnp.zeros((256, 128), F32)
            return c

        lax.fori_loop(0, 128, clear, 0)

    half = lax.broadcasted_iota(jnp.int32, (32, 128), 1) // 64

    @pl.when(i < FILL_STEPS)
    def _():
        def group(g, c):
            for s in range(8):
                slot = (i * STEP_GROUPS + g) * 8 + s
                first = rows_ref[slot] * BS
                q = slots_ref[slot]
                side = jnp.where(slot < live, q % 2, 2)
                two = vals_ref[g, pl.ds(s, 32, stride=8), :]
                turned = pltpu.roll(two, 64, 1)
                even = jnp.where(half == side, jnp.where(half == 0, two, turned), 0.0)
                odd = jnp.where(half == side, jnp.where(half == 0, turned, two), 0.0)
                dense[q // 2, pl.ds(first, 32, stride=2), :] += even
                dense[q // 2, pl.ds(first + 1, 32, stride=2), :] += odd
            return c

        left = (live + 7) // 8 - i * STEP_GROUPS
        lax.fori_loop(0, jnp.clip(left, 0, STEP_GROUPS), group, 0)

    @pl.when(i >= FILL_STEPS)
    def _():
        first = pl.multiple_of((i - FILL_STEPS) * CHUNK, CHUNK)
        for j in range(16):
            high, low = split(dense[j, pl.ds(first, CHUNK), :])
            hi_ref[:, j * 128 : (j + 1) * 128] = high
            lo_ref[:, j * 128 : (j + 1) * 128] = low


def dense_of(values, rel_rows, slots, live):
    grid = FILL_STEPS + CHUNKS
    out = pl.BlockSpec((CHUNK, SIDE), lambda i, *_: (jnp.maximum(i - FILL_STEPS, 0), 0))
    return pl.pallas_call(
        dense_kernel,
        grid_spec=pltpu.PrefetchScalarGridSpec(
            num_scalar_prefetch=3,
            grid=(grid,),
            in_specs=[pl.BlockSpec((STEP_GROUPS, 256, 128), lambda i, *_: (jnp.minimum(i, FILL_STEPS - 1), 0, 0))],
            out_specs=[out, out],
            scratch_shapes=[pltpu.VMEM((16, SIDE, 128), F32)],
        ),
        out_shape=[jax.ShapeDtypeStruct((SIDE, SIDE), BF16)] * 2,
        compiler_params=pltpu.CompilerParams(vmem_limit_bytes=56 * MIB),
        cost_estimate=pl.CostEstimate(flops=10**7, bytes_accessed=50 * 10**6, transcendentals=0),
        name="dense",
    )(rel_rows, slots, live, values)


def fetches(columns, i, hi_any, lo_any, hi, lo, sems):
    here = pl.ds(pl.multiple_of(i * CHUNK, CHUNK), CHUNK)
    at = (slice(None), here) if columns else (here, slice(None))
    return [
        pltpu.make_async_copy(src.at[at], dst.at[at], sems.at[n, i])
        for n, (src, dst) in enumerate(((hi_any, hi), (lo_any, lo)))
    ]


def begin_fetches(columns, *refs):
    def begin(i, c):
        for copy in fetches(columns, i, *refs):
            copy.start()
        return c

    lax.fori_loop(0, CHUNKS, begin, 0)


def forward_kernel(whole, need_ref, hi_any, lo_any, cols, keep, send, hi, lo, xc, sems):
    begin_fetches(False, hi_any, lo_any, hi, lo, sems)

    def column(p, c):
        for k in range(KS):
            if whole:
                first = jnp.minimum(need_ref[p * KS + k], RB - 1) * BS
                block = cols[p, pl.ds(pl.multiple_of(first, BS), BS), :]
            else:
                block = cols[p, k * BS : (k + 1) * BS, :]
            high, low = split(block)
            here = pl.ds(pl.multiple_of((p * KS + k) * BS, BS), BS)
            xc[here, 0:128] = high
            xc[here, 128:256] = low
        return c

    lax.fori_loop(0, N_COL, column, 0)

    def chunk(i, c):
        here = pl.ds(pl.multiple_of(i * CHUNK, CHUNK), CHUNK)
        x = xc[...]
        for copy in fetches(False, i, hi_any, lo_any, hi, lo, sems):
            copy.wait()
        out = jnp.dot(hi[here, :], x, preferred_element_type=F32) + jnp.dot(lo[here, :], x, preferred_element_type=F32)
        out = out[:, :128] + out[:, 128:]

        @pl.when(i < 4)
        def _():
            keep[jnp.minimum(i, 3)] = out

        @pl.when(i >= 4)
        def _():
            send[jnp.maximum(i - 4, 0)] = out

        return c

    lax.fori_loop(0, CHUNKS, chunk, 0)


def backward_kernel(hi_any, lo_any, own, z1, z2, z3, far, extra, pay, hi, lo, xr, sems):
    begin_fetches(True, hi_any, lo_any, hi, lo, sems)
    for c in range(CHUNKS):
        piece = (own, z1, z2, z3)[c][...] if c < 4 else far[(c - 4) * CHUNK : (c - 3) * CHUNK, :]
        high, low = split(piece.T)
        xr[0:128, c * CHUNK : (c + 1) * CHUNK] = high
        xr[128:256, c * CHUNK : (c + 1) * CHUNK] = low

    def chunk(j, c):
        here = pl.ds(pl.multiple_of(j * CHUNK, CHUNK), CHUNK)
        v = xr[...]
        for copy in fetches(True, j, hi_any, lo_any, hi, lo, sems):
            copy.wait()
        out = jnp.dot(v, hi[:, here], preferred_element_type=F32) + jnp.dot(v, lo[:, here], preferred_element_type=F32)
        out = (out[:128] + out[128:]).T
        for q in range(2):
            p = j * 2 + q
            pay[p, 0:128, :] = out[q * 128 : (q + 1) * 128]
            pay[p, 128:, :] = extra[p]
        return c

    lax.fori_loop(0, CHUNKS, chunk, 0)


VMEM = pl.BlockSpec(memory_space=pltpu.VMEM)
ANYWHERE = pl.BlockSpec(memory_space=pl.ANY)
PRODUCT = {
    "compiler_params": pltpu.CompilerParams(vmem_limit_bytes=50 * MIB),
    "cost_estimate": pl.CostEstimate(flops=4 * 10**9, bytes_accessed=20 * 10**6, transcendentals=0),
}


def forward(whole, need, hi, lo, cols):
    return pl.pallas_call(
        functools.partial(forward_kernel, whole),
        in_specs=[pl.BlockSpec(memory_space=pltpu.SMEM), ANYWHERE, ANYWHERE, VMEM],
        out_specs=[VMEM] * 2,
        scratch_shapes=[
            pltpu.VMEM((SIDE, SIDE), BF16),
            pltpu.VMEM((SIDE, SIDE), BF16),
            pltpu.VMEM((SIDE, 256), BF16),
            pltpu.SemaphoreType.DMA((2, CHUNKS)),
        ],
        out_shape=[jax.ShapeDtypeStruct((4, ROWS, NB), F32)] * 2,
        name="forward",
        **PRODUCT,
    )(need, hi, lo, cols)


def backward(hi, lo, pieces, extra):
    return pl.pallas_call(
        backward_kernel,
        in_specs=[ANYWHERE, ANYWHERE] + [VMEM] * 6,
        out_specs=VMEM,
        scratch_shapes=[
            pltpu.VMEM((SIDE, SIDE), BF16),
            pltpu.VMEM((SIDE, SIDE), BF16),
            pltpu.VMEM((256, SIDE), BF16),
            pltpu.SemaphoreType.DMA((2, CHUNKS)),
        ],
        out_shape=jax.ShapeDtypeStruct((N_COL, 128 + extra.shape[1], NB), F32),
        name="backward",
        **PRODUCT,
    )(hi, lo, *pieces, extra)


def image_of(v, deg, s0, s1, s2, s3, arrived, needs):
    sums = s0[...] + s1[...] + s2[...] + s3[...]

    def peer(p, parts):
        for q in range(KS):
            block = arrived[p, q * BS : (q + 1) * BS, :]
            which = needs[p, q : q + 1, :]
            parts = tuple(parts[k] + jnp.where(which == float(k), block, 0.0) for k in range(RB))
        return parts

    zero = jnp.zeros((BS, NB), F32)
    parts = lax.fori_loop(0, N_COL, peer, (zero,) * RB)
    return (deg[...] - SHIFT) * v[...] - sums - jnp.concatenate(parts, axis=0)


def first_kernel(v, deg, s0, s1, s2, s3, arrived, image, pay, needs):
    needs[...] = arrived[:, 128:136, :]
    y = image_of(v, deg, s0, s1, s2, s3, arrived, needs)
    image[...] = y
    for p in range(N_COL):
        for q in range(KS):
            which = needs[p, q : q + 1, :]
            block = jnp.zeros((BS, NB), F32)
            for k in range(RB):
                block = jnp.where(which == float(k), image[k * BS : (k + 1) * BS, :], block)
            pay[p, q * BS : (q + 1) * BS, :] = block
    x = v[...]
    xt, yt = x.T, y.T
    for at, gram in ((128, mm(xt, x)), (136, mm(xt, y)), (144, mm(yt, y))):
        gram = gram * (1.0 / NROWS)
        for p in range(N_COL):
            pay[p, at : at + 8, :] = gram[8 * p : 8 * p + 8, :]


def first_image(v, deg, sums, arrived):
    return pl.pallas_call(
        first_kernel,
        out_shape=[
            jax.ShapeDtypeStruct((ROWS, NB), F32),
            jax.ShapeDtypeStruct((N_COL, 128 + SUMS, NB), F32),
            jax.ShapeDtypeStruct((N_COL, 8, NB), F32),
        ],
        compiler_params=pltpu.CompilerParams(vmem_limit_bytes=32 * MIB),
        name="first_image",
    )(v, deg, *sums, arrived)


PANEL = 64
WINDOW = 8


def factor(a):
    z = eye()
    row = lax.broadcasted_iota(jnp.int32, (PANEL, NB), 0)
    uppers, inverses = [], []
    for b in range(NB // PANEL):
        pa, pz = a[:PANEL], z[:PANEL]
        da = dz = jnp.zeros((PANEL, NB), F32)
        for t in range(0, PANEL, WINDOW):
            k = b * PANEL + t
            here = range(WINDOW)
            cols = [jnp.broadcast_to(pa[:, k + i : k + i + 1], (PANEL, NB)) for i in here]
            ra = [pa[t + i : t + i + 1, :] for i in here]
            rz = [pz[t + i : t + i + 1, :] for i in here]
            tops = [[cols[j][t + i : t + i + 1, :] for j in here] for i in here]
            for i in here:
                root = lax.rsqrt(tops[i][i])
                inverse = root * root
                for j in range(i + 1, WINDOW):
                    times = tops[i][j] * inverse
                    ra[j] = ra[j] - times * ra[i]
                    rz[j] = rz[j] - times * rz[i]
                    cols[j] = cols[j] - times * cols[i]
                    for m in range(j, WINDOW):
                        tops[j][m] = tops[j][m] - times * tops[i][m]
                da = jnp.where(row == t + i, ra[i] * root, da)
                dz = jnp.where(row == t + i, rz[i] * root, dz)
                cols[i] = cols[i] * inverse
            for i in here:
                pa = pa - cols[i] * ra[i]
                pz = pz - cols[i] * rz[i]
        uppers.append(da)
        inverses.append(dz)
        if b < NB // PANEL - 1:
            left = da.T[(b + 1) * PANEL :, :]
            a = a[PANEL:] - mm(left, da)
            z = z[PANEL:] - mm(left, dz)
    lane = lax.broadcasted_iota(jnp.int32, (NB, NB), 1)
    sub = lax.broadcasted_iota(jnp.int32, (NB, NB), 0)
    return jnp.where(lane >= sub, jnp.concatenate(uppers, axis=0), 0.0), jnp.concatenate(inverses, axis=0)


def eye():
    return jnp.where(
        lax.broadcasted_iota(jnp.int32, (NB, NB), 0) == lax.broadcasted_iota(jnp.int32, (NB, NB), 1), 1.0, 0.0
    )


def second_kernel(x_ref, y_ref, deg, s0, s1, s2, s3, arrived, needs, grams, alpha, beta, v0_ref, v1_ref, w_ref, gram):
    y2 = image_of(y_ref, deg, s0, s1, s2, s3, arrived, needs)
    xx, xy, yy = (
        jnp.concatenate([grams[p, at : at + 8, :] for p in range(N_COL)], axis=0) for at in (0, 8, 16)
    )
    x, y = x_ref[...], y_ref[...]
    _, inv0 = factor(xx)
    a0 = mm(mm(inv0, xy), inv0, 1, 1)
    b0 = mm(mm(inv0, yy), inv0, 1, 1)
    alpha[...] = a0 + SHIFT * eye()
    upper1, inv1 = factor(b0 - mm(a0, a0, 0, 0))
    beta[...] = upper1
    v0 = mm(x, inv0, 1, 1)
    t = mm(inv0, inv1, 0, 1)
    u = mm(mm(inv0, a0, 0, 0), inv1, 1, 1)
    v1 = mm(y, t) - mm(x, u)
    w = mm(y2, t) - mm(y, u)
    v0_ref[...], v1_ref[...], w_ref[...] = v0, v1, w
    gram[0:128, :] = mm(v0.T, w) * (1.0 / NROWS)
    gram[128:256, :] = mm(v1.T, w) * (1.0 / NROWS)
    gram[256:384, :] = mm(w.T, w) * (1.0 / NROWS)


def second_image(x, y, deg, sums, arrived, needs, grams):
    square = jax.ShapeDtypeStruct((NB, NB), F32)
    owned = jax.ShapeDtypeStruct((ROWS, NB), F32)
    return pl.pallas_call(
        second_kernel,
        out_shape=[square, square, owned, owned, owned, jax.ShapeDtypeStruct((3 * NB, NB), F32)],
        compiler_params=pltpu.CompilerParams(vmem_limit_bytes=32 * MIB),
        name="second_image",
    )(x, y, deg, *sums, arrived, needs, grams)


def last_kernel(v0, v1, w, gram, alpha0, beta0, alphas, betas, basis):
    a0, a1, b = gram[0:128, :], gram[128:256, :], gram[256:384, :]
    upper, inv = factor(b - mm(a0, a0, 0, 0) - mm(a1, a1, 0, 0))
    alphas[0], betas[0] = alpha0[...], beta0[...]
    alphas[1] = a1 + SHIFT * eye()
    betas[1] = upper
    w2 = w[...] - mm(v0[...], a0) - mm(v1[...], a1)
    basis[...] = mm(w2, inv, 1, 1)


def last_block(*args):
    pair = jax.ShapeDtypeStruct((2, NB, NB), F32)
    return pl.pallas_call(
        last_kernel,
        out_shape=[pair, pair, jax.ShapeDtypeStruct((ROWS, NB), F32)],
        compiler_params=pltpu.CompilerParams(vmem_limit_bytes=32 * MIB),
        name="last_block",
    )(*args)


CORE = [(i, i ^ 1) for i in range(N_ROW)]


def along_z(k):
    return [(i, ((i // 2) ^ k) * 2 + i % 2) for i in range(N_ROW)]


def along_x(k):
    return [(i, ((i // 4) ^ k) * 4 + i % 4) for i in range(N_COL)]


def along_y(k):
    return [(i, (i // 4) * 4 + ((i % 4) ^ k)) for i in range(N_COL)]


def row_pieces(own, *after):
    three = [lax.ppermute(own, "row", along_z(k)) for k in (1, 2, 3)]
    if after:
        *three, _ = lax.optimization_barrier((*three, *after))
    far = lax.ppermute(jnp.concatenate([own, *three]), "row", CORE)
    return [own, *three, far]


def row_sums(keep, send):
    other = lax.ppermute(send, "row", CORE)
    parts = [keep[k] + other[k] for k in range(4)]
    return [parts[0]] + [lax.ppermute(parts[k], "row", along_z(k)) for k in (1, 2, 3)]


def swap(x):
    return lax.all_to_all(x, "col", 0, 0)


def ring_sum(x, axis, shift):
    return x + sum(lax.ppermute(x, axis, shift(k)) for k in (1, 2, 3))


def sum_all(x):
    core = lax.axis_index("row") % 2
    n = x.shape[0] // 2
    here = jnp.where(core == 0, x[:n], x[n:])
    there = jnp.where(core == 0, x[n:], x[:n])
    here = here + lax.ppermute(there, "row", CORE)
    here = ring_sum(here, "row", along_z)
    here = ring_sum(here, "col", along_x)
    here = ring_sum(here, "col", along_y)
    other = lax.ppermute(here, "row", CORE)
    return jnp.concatenate([jnp.where(core == 0, here, other), jnp.where(core == 0, other, here)])


def on_device(start_block, degree, block_values, block_rows, block_slots, need_lists, live_blocks):
    row = lax.axis_index("row")
    z, core = row // 2, row % 2
    owner, k = block_rows // RB, block_rows % RB
    rel_rows = (((owner % 2) ^ core) * 4 + ((owner // 2) ^ z)) * RB + k
    need = need_lists.reshape(-1)
    needs_out = jnp.broadcast_to(
        jnp.pad(need_lists.astype(F32), ((0, 0), (0, 8 - KS)))[:, :, None], (N_COL, 8, NB)
    )
    deg = jnp.broadcast_to(degree[:, None], (ROWS, NB))
    values = block_values.reshape(GROUPS, 8, 32, 128).transpose(0, 2, 1, 3).reshape(GROUPS, 256, 128)

    cols = swap(jnp.broadcast_to(start_block[None], (N_COL, ROWS, NB)))
    hi, lo = dense_of(values, rel_rows, block_slots, live_blocks)
    pieces = row_pieces(start_block, hi)
    back = swap(backward(hi, lo, pieces, needs_out))
    sums = row_sums(*forward(True, need, hi, lo, cols))
    y, pay, needs = first_image(start_block, deg, sums, back)

    cols = swap(pay)
    pieces = row_pieces(y)
    back = backward(hi, lo, pieces, jnp.zeros((N_COL, 8, NB), F32))
    cols, back = lax.optimization_barrier((cols, back))
    back = swap(back)
    keep, send = forward(False, need, hi, lo, cols)
    cols, keep, send = lax.optimization_barrier((cols, keep, send))
    part = cols[:, 128:, :].sum(0)
    part = part + lax.ppermute(part, "row", CORE)
    part = ring_sum(part, "row", along_z)
    grams = swap(jnp.broadcast_to(part[None], (N_COL, SUMS, NB)))
    sums = row_sums(keep, send)
    alpha, beta, v0, v1, w, gram = second_image(start_block, y, deg, sums, back, needs, grams)
    return tuple(last_block(v0, v1, w, sum_all(gram), alpha, beta))


def solution(mesh):
    return jax.shard_map(
        on_device,
        mesh=mesh,
        in_specs=(
            P(("row", "col"), None),
            P(("row", "col")),
            P(("row", "col"), None),
            P(("row", "col")),
            P(("row", "col")),
            P(("row", "col"), None),
            P(("row", "col")),
        ),
        out_specs=(P(), P(), P(("row", "col"), None)),
        check_vma=False,
    )
```

```python
import functools

import jax
import jax.numpy as jnp
from jax import lax
from jax.experimental import pallas as pl
from jax.experimental.pallas import tpu as pltpu
from jax.sharding import PartitionSpec as P

BS = 64
RB = 4
KS = 2
NB = 128
ROWS = RB * BS
N_ROW = 8
N_COL = 16
NROWS = ROWS * N_ROW * N_COL
CAP = 384
SIDE = 2048
SHIFT = 4.0
GROUPS = CAP // 8
STEP_GROUPS = 6
FILL_STEPS = GROUPS // STEP_GROUPS
CHUNK = 256
CHUNKS = SIDE // CHUNK
PART = NB // N_ROW
SLICE = 3 * PART

HIGH = lax.Precision.HIGHEST
F32, BF16 = jnp.float32, jnp.bfloat16
MIB = 2**20


def mm(a, b, ca=1, cb=0):
    return lax.dot_general(a, b, (((ca,), (cb,)), ((), ())), precision=HIGH, preferred_element_type=F32)


def split(x):
    high = x.astype(BF16)
    return high, (x - high.astype(F32)).astype(BF16)


def dense_kernel(rows_ref, slots_ref, live_ref, vals_ref, hi_ref, lo_ref, dense):
    i = pl.program_id(0)
    live = live_ref[0]

    @pl.when(i == 0)
    def _():
        def clear(t, c):
            dense[t // 8, pl.ds(pl.multiple_of((t % 8) * 256, 256), 256), :] = jnp.zeros((256, 128), F32)
            return c

        lax.fori_loop(0, 128, clear, 0)

    half = lax.broadcasted_iota(jnp.int32, (32, 128), 1) // 64

    @pl.when(i < FILL_STEPS)
    def _():
        def group(g, c):
            for s in range(8):
                slot = (i * STEP_GROUPS + g) * 8 + s
                first = rows_ref[slot] * BS
                q = slots_ref[slot]
                side = jnp.where(slot < live, q % 2, 2)
                two = vals_ref[g, pl.ds(s, 32, stride=8), :]
                turned = pltpu.roll(two, 64, 1)
                even = jnp.where(half == side, jnp.where(half == 0, two, turned), 0.0)
                odd = jnp.where(half == side, jnp.where(half == 0, turned, two), 0.0)
                dense[q // 2, pl.ds(first, 32, stride=2), :] += even
                dense[q // 2, pl.ds(first + 1, 32, stride=2), :] += odd
            return c

        left = (live + 7) // 8 - i * STEP_GROUPS
        lax.fori_loop(0, jnp.clip(left, 0, STEP_GROUPS), group, 0)

    @pl.when(i >= FILL_STEPS)
    def _():
        first = pl.multiple_of((i - FILL_STEPS) * CHUNK, CHUNK)
        for j in range(16):
            high, low = split(dense[j, pl.ds(first, CHUNK), :])
            hi_ref[:, j * 128 : (j + 1) * 128] = high
            lo_ref[:, j * 128 : (j + 1) * 128] = low


def dense_of(values, rel_rows, slots, live):
    grid = FILL_STEPS + CHUNKS
    out = pl.BlockSpec((CHUNK, SIDE), lambda i, *_: (jnp.maximum(i - FILL_STEPS, 0), 0))
    return pl.pallas_call(
        dense_kernel,
        grid_spec=pltpu.PrefetchScalarGridSpec(
            num_scalar_prefetch=3,
            grid=(grid,),
            in_specs=[pl.BlockSpec((STEP_GROUPS, 256, 128), lambda i, *_: (jnp.minimum(i, FILL_STEPS - 1), 0, 0))],
            out_specs=[out, out],
            scratch_shapes=[pltpu.VMEM((16, SIDE, 128), F32)],
        ),
        out_shape=[jax.ShapeDtypeStruct((SIDE, SIDE), BF16)] * 2,
        compiler_params=pltpu.CompilerParams(vmem_limit_bytes=56 * MIB),
        cost_estimate=pl.CostEstimate(flops=10**7, bytes_accessed=50 * 10**6, transcendentals=0),
        name="dense",
    )(rel_rows, slots, live, values)


def fetches(columns, i, hi_any, lo_any, hi, lo, sems):
    here = pl.ds(pl.multiple_of(i * CHUNK, CHUNK), CHUNK)
    at = (slice(None), here) if columns else (here, slice(None))
    return [
        pltpu.make_async_copy(src.at[at], dst.at[at], sems.at[n, i])
        for n, (src, dst) in enumerate(((hi_any, hi), (lo_any, lo)))
    ]


def begin_fetches(columns, *refs):
    def begin(i, c):
        for copy in fetches(columns, i, *refs):
            copy.start()
        return c

    lax.fori_loop(0, CHUNKS, begin, 0)


def forward_kernel(whole, need_ref, hi_any, lo_any, cols, keep, send, hi, lo, xc, sems):
    begin_fetches(False, hi_any, lo_any, hi, lo, sems)

    def column(p, c):
        for k in range(KS):
            if whole:
                first = jnp.minimum(need_ref[p * KS + k], RB - 1) * BS
                block = cols[p, pl.ds(pl.multiple_of(first, BS), BS), :]
            else:
                block = cols[p, k * BS : (k + 1) * BS, :]
            high, low = split(block)
            here = pl.ds(pl.multiple_of((p * KS + k) * BS, BS), BS)
            xc[here, 0:128] = high
            xc[here, 128:256] = low
        return c

    lax.fori_loop(0, N_COL, column, 0)

    def chunk(i, c):
        here = pl.ds(pl.multiple_of(i * CHUNK, CHUNK), CHUNK)
        x = xc[...]
        for copy in fetches(False, i, hi_any, lo_any, hi, lo, sems):
            copy.wait()
        out = jnp.dot(hi[here, :], x, preferred_element_type=F32) + jnp.dot(lo[here, :], x, preferred_element_type=F32)
        out = out[:, :128] + out[:, 128:]

        @pl.when(i < 4)
        def _():
            keep[jnp.minimum(i, 3)] = out

        @pl.when(i >= 4)
        def _():
            send[jnp.maximum(i - 4, 0)] = out

        return c

    lax.fori_loop(0, CHUNKS, chunk, 0)


def backward_kernel(hi_any, lo_any, own, z1, z2, z3, far, extra, pay, hi, lo, xr, sems):
    begin_fetches(True, hi_any, lo_any, hi, lo, sems)
    for c in range(CHUNKS):
        piece = (own, z1, z2, z3)[c][0:ROWS, :] if c < 4 else far[(c - 4) * CHUNK : (c - 3) * CHUNK, :]
        high, low = split(piece.T)
        xr[0:128, c * CHUNK : (c + 1) * CHUNK] = high
        xr[128:256, c * CHUNK : (c + 1) * CHUNK] = low

    def chunk(j, c):
        here = pl.ds(pl.multiple_of(j * CHUNK, CHUNK), CHUNK)
        v = xr[...]
        for copy in fetches(True, j, hi_any, lo_any, hi, lo, sems):
            copy.wait()
        out = jnp.dot(v, hi[:, here], preferred_element_type=F32) + jnp.dot(v, lo[:, here], preferred_element_type=F32)
        out = (out[:128] + out[128:]).T
        for q in range(2):
            p = j * 2 + q
            pay[p, 0:128, :] = out[q * 128 : (q + 1) * 128]
            pay[p, 128:, :] = extra[p] if len(extra.shape) == 3 else extra[...]
        return c

    lax.fori_loop(0, CHUNKS, chunk, 0)


VMEM = pl.BlockSpec(memory_space=pltpu.VMEM)
ANYWHERE = pl.BlockSpec(memory_space=pl.ANY)
PRODUCT = {
    "compiler_params": pltpu.CompilerParams(vmem_limit_bytes=50 * MIB),
    "cost_estimate": pl.CostEstimate(flops=10**6, bytes_accessed=10**5, transcendentals=0),
}


def forward(whole, need, hi, lo, cols):
    return pl.pallas_call(
        functools.partial(forward_kernel, whole),
        in_specs=[pl.BlockSpec(memory_space=pltpu.SMEM), ANYWHERE, ANYWHERE, VMEM],
        out_specs=[VMEM] * 2,
        scratch_shapes=[
            pltpu.VMEM((SIDE, SIDE), BF16),
            pltpu.VMEM((SIDE, SIDE), BF16),
            pltpu.VMEM((SIDE, 256), BF16),
            pltpu.SemaphoreType.DMA((2, CHUNKS)),
        ],
        out_shape=[jax.ShapeDtypeStruct((4, ROWS, NB), F32)] * 2,
        name="forward",
        **PRODUCT,
    )(need, hi, lo, cols)


def backward(hi, lo, pieces, extra):
    return pl.pallas_call(
        backward_kernel,
        in_specs=[ANYWHERE, ANYWHERE] + [VMEM] * 6,
        out_specs=VMEM,
        scratch_shapes=[
            pltpu.VMEM((SIDE, SIDE), BF16),
            pltpu.VMEM((SIDE, SIDE), BF16),
            pltpu.VMEM((256, SIDE), BF16),
            pltpu.SemaphoreType.DMA((2, CHUNKS)),
        ],
        out_shape=jax.ShapeDtypeStruct((N_COL, 128 + extra.shape[-2], NB), F32),
        name="backward",
        **PRODUCT,
    )(hi, lo, *pieces, extra)


def image_of(v, deg, s0, s1, s2, s3, arrived, needs):
    sums = s0[...] + s1[...] + s2[...] + s3[...]

    def peer(p, parts):
        for q in range(KS):
            block = arrived[p, q * BS : (q + 1) * BS, :]
            which = needs[p, q : q + 1, :]
            parts = tuple(parts[k] + jnp.where(which == float(k), block, 0.0) for k in range(RB))
        return parts

    zero = jnp.zeros((BS, NB), F32)
    parts = lax.fori_loop(0, N_COL, peer, (zero,) * RB)
    return (deg[...] - SHIFT) * v[...] - sums - jnp.concatenate(parts, axis=0)


def first_kernel(v, deg, s0, s1, s2, s3, arrived, image, pay, needs, slices):
    needs[...] = arrived[:, 128:136, :]
    y = image_of(v, deg, s0, s1, s2, s3, arrived, needs)
    image[...] = y
    for p in range(N_COL):
        for q in range(KS):
            which = needs[p, q : q + 1, :]
            block = jnp.zeros((BS, NB), F32)
            for k in range(RB):
                block = jnp.where(which == float(k), image[k * BS : (k + 1) * BS, :], block)
            pay[p, q * BS : (q + 1) * BS, :] = block
    x = v[...]
    xt, yt = x.T, y.T
    for n, gram in enumerate((mm(xt, x), mm(xt, y), mm(yt, y))):
        gram = gram * (1.0 / NROWS)
        for r in range(N_ROW):
            slices[r, n * PART : (n + 1) * PART, :] = gram[r * PART : (r + 1) * PART, :]


def first_image(v, deg, sums, arrived):
    return pl.pallas_call(
        first_kernel,
        out_shape=[
            jax.ShapeDtypeStruct((ROWS, NB), F32),
            jax.ShapeDtypeStruct((N_COL, 128, NB), F32),
            jax.ShapeDtypeStruct((N_COL, 8, NB), F32),
            jax.ShapeDtypeStruct((N_ROW, SLICE, NB), F32),
        ],
        compiler_params=pltpu.CompilerParams(vmem_limit_bytes=32 * MIB),
        name="first_image",
    )(v, deg, *sums, arrived)


PANEL = 64
WINDOW = 8


def factor(a):
    z = eye()
    row = lax.broadcasted_iota(jnp.int32, (PANEL, NB), 0)
    uppers, inverses = [], []
    for b in range(NB // PANEL):
        pa, pz = a[:PANEL], z[:PANEL]
        da = dz = jnp.zeros((PANEL, NB), F32)
        for t in range(0, PANEL, WINDOW):
            k = b * PANEL + t
            here = range(WINDOW)
            cols = [jnp.broadcast_to(pa[:, k + i : k + i + 1], (PANEL, NB)) for i in here]
            ra = [pa[t + i : t + i + 1, :] for i in here]
            rz = [pz[t + i : t + i + 1, :] for i in here]
            tops = [[cols[j][t + i : t + i + 1, :] for j in here] for i in here]
            for i in here:
                root = lax.rsqrt(tops[i][i])
                inverse = root * root
                for j in range(i + 1, WINDOW):
                    times = tops[i][j] * inverse
                    ra[j] = ra[j] - times * ra[i]
                    rz[j] = rz[j] - times * rz[i]
                    cols[j] = cols[j] - times * cols[i]
                    for m in range(j, WINDOW):
                        tops[j][m] = tops[j][m] - times * tops[i][m]
                da = jnp.where(row == t + i, ra[i] * root, da)
                dz = jnp.where(row == t + i, rz[i] * root, dz)
                cols[i] = cols[i] * inverse
            for i in here:
                pa = pa - cols[i] * ra[i]
                pz = pz - cols[i] * rz[i]
        uppers.append(da)
        inverses.append(dz)
        if b < NB // PANEL - 1:
            left = da.T[(b + 1) * PANEL :, :]
            a = a[PANEL:] - mm(left, da)
            z = z[PANEL:] - mm(left, dz)
    lane = lax.broadcasted_iota(jnp.int32, (NB, NB), 1)
    sub = lax.broadcasted_iota(jnp.int32, (NB, NB), 0)
    return jnp.where(lane >= sub, jnp.concatenate(uppers, axis=0), 0.0), jnp.concatenate(inverses, axis=0)


def eye():
    return jnp.where(
        lax.broadcasted_iota(jnp.int32, (NB, NB), 0) == lax.broadcasted_iota(jnp.int32, (NB, NB), 1), 1.0, 0.0
    )


def image_kernel(v, deg, s0, s1, s2, s3, arrived, needs, image):
    image[...] = image_of(v, deg, s0, s1, s2, s3, arrived, needs)


def image(v, deg, sums, arrived, needs):
    return pl.pallas_call(
        image_kernel,
        out_shape=jax.ShapeDtypeStruct((ROWS, NB), F32),
        compiler_params=pltpu.CompilerParams(vmem_limit_bytes=32 * MIB),
        name="image",
    )(v, deg, *sums, arrived, needs)


def second_kernel(place, x_ref, y_ref, y2_ref, near, far, alpha, beta, v0_ref, v1_ref, w_ref, gram, grams):
    z, core = place[0], place[1]
    for k in range(4):
        here = slice(k * SLICE, (k + 1) * SLICE)
        grams[(z ^ k) * 2 + core] = near[here, :]
        grams[(z ^ k) * 2 + (1 - core)] = far[here, :]
    y2 = y2_ref[...]
    xx, xy, yy = (
        jnp.concatenate([grams[r, n * PART : (n + 1) * PART, :] for r in range(N_ROW)], axis=0) for n in range(3)
    )
    x, y = x_ref[...], y_ref[...]
    _, inv0 = factor(xx)
    a0 = mm(mm(inv0, xy), inv0, 1, 1)
    b0 = mm(mm(inv0, yy), inv0, 1, 1)
    alpha[...] = a0 + SHIFT * eye()
    upper1, inv1 = factor(b0 - mm(a0, a0, 0, 0))
    beta[...] = upper1
    v0 = mm(x, inv0, 1, 1)
    t = mm(inv0, inv1, 0, 1)
    u = mm(mm(inv0, a0, 0, 0), inv1, 1, 1)
    v1 = mm(y, t) - mm(x, u)
    w = mm(y2, t) - mm(y, u)
    v0_ref[...], v1_ref[...], w_ref[...] = v0, v1, w
    gram[0:128, :] = mm(v0.T, w) * (1.0 / NROWS)
    gram[128:256, :] = mm(v1.T, w) * (1.0 / NROWS)
    gram[256:384, :] = mm(w.T, w) * (1.0 / NROWS)


def second_block(*args):
    square = jax.ShapeDtypeStruct((NB, NB), F32)
    owned = jax.ShapeDtypeStruct((ROWS, NB), F32)
    return pl.pallas_call(
        second_kernel,
        in_specs=[pl.BlockSpec(memory_space=pltpu.SMEM)] + [VMEM] * 5,
        out_specs=[VMEM] * 6,
        out_shape=[square, square, owned, owned, owned, jax.ShapeDtypeStruct((3 * NB, NB), F32)],
        scratch_shapes=[pltpu.VMEM((N_ROW, SLICE, NB), F32)],
        compiler_params=pltpu.CompilerParams(vmem_limit_bytes=32 * MIB),
        name="second_block",
    )(*args)


def last_kernel(v0, v1, w, gram, alpha0, beta0, alphas, betas, basis):
    a0, a1, b = gram[0:128, :], gram[128:256, :], gram[256:384, :]
    upper, inv = factor(b - mm(a0, a0, 0, 0) - mm(a1, a1, 0, 0))
    alphas[0], betas[0] = alpha0[...], beta0[...]
    alphas[1] = a1 + SHIFT * eye()
    betas[1] = upper
    w2 = w[...] - mm(v0[...], a0) - mm(v1[...], a1)
    basis[...] = mm(w2, inv, 1, 1)


def last_block(*args):
    pair = jax.ShapeDtypeStruct((2, NB, NB), F32)
    return pl.pallas_call(
        last_kernel,
        out_shape=[pair, pair, jax.ShapeDtypeStruct((ROWS, NB), F32)],
        compiler_params=pltpu.CompilerParams(vmem_limit_bytes=32 * MIB),
        name="last_block",
    )(*args)


CORE = [(i, i ^ 1) for i in range(N_ROW)]


def along_z(k):
    return [(i, ((i // 2) ^ k) * 2 + i % 2) for i in range(N_ROW)]


def along_x(k):
    return [(i, ((i // 4) ^ k) * 4 + i % 4) for i in range(N_COL)]


def along_y(k):
    return [(i, (i // 4) * 4 + ((i % 4) ^ k)) for i in range(N_COL)]


def row_pieces(own, *after):
    three = [lax.ppermute(own, "row", along_z(k)) for k in (1, 2, 3)]
    if after:
        *three, _ = lax.optimization_barrier((*three, *after))
    far = lax.ppermute(jnp.concatenate([own, *three]), "row", CORE)
    return [own, *three, far]


def row_pieces_and_sums(own, slices, z, core):
    chips = slices.reshape(N_ROW // 2, 2 * SLICE, NB)
    three = [lax.ppermute(jnp.concatenate([own, chips[z ^ k]]), "row", along_z(k)) for k in (1, 2, 3)]
    a, b, c = (got[ROWS:] for got in three)
    pair = ((chips[z] + a) + (b + c)).reshape(2, SLICE, NB)
    far = lax.ppermute(jnp.concatenate([own, *(got[:ROWS] for got in three), pair[1 - core]]), "row", CORE)
    return [own, *three, far], pair[core] + far[4 * ROWS :]


def row_sums(keep, send):
    other = lax.ppermute(send, "row", CORE)
    parts = [keep[k] + other[k] for k in range(4)]
    return [parts[0]] + [lax.ppermute(parts[k], "row", along_z(k)) for k in (1, 2, 3)]


def swap(x):
    return lax.all_to_all(x, "col", 0, 0)


def ring_sum(x, axis, shift):
    a, b, c = (lax.ppermute(x, axis, shift(k)) for k in (1, 2, 3))
    return (x + a) + (b + c)


def sum_all(x):
    core = lax.axis_index("row") % 2
    n = x.shape[0] // 2
    here = jnp.where(core == 0, x[:n], x[n:])
    there = jnp.where(core == 0, x[n:], x[:n])
    here = here + lax.ppermute(there, "row", CORE)
    here = ring_sum(here, "row", along_z)
    here = ring_sum(here, "col", along_x)
    here = ring_sum(here, "col", along_y)
    other = lax.ppermute(here, "row", CORE)
    return jnp.concatenate([jnp.where(core == 0, here, other), jnp.where(core == 0, other, here)])


def on_device(start_block, degree, block_values, block_rows, block_slots, need_lists, live_blocks):
    row = lax.axis_index("row")
    z, core = row // 2, row % 2
    owner, k = block_rows // RB, block_rows % RB
    rel_rows = (((owner % 2) ^ core) * 4 + ((owner // 2) ^ z)) * RB + k
    need = need_lists.reshape(-1)
    needs_out = jnp.broadcast_to(
        jnp.pad(need_lists.astype(F32), ((0, 0), (0, 8 - KS)))[:, :, None], (N_COL, 8, NB)
    )
    deg = jnp.broadcast_to(degree[:, None], (ROWS, NB))
    values = block_values.reshape(GROUPS, 8, 32, 128).transpose(0, 2, 1, 3).reshape(GROUPS, 256, 128)

    cols = swap(jnp.broadcast_to(start_block[None], (N_COL, ROWS, NB)))
    hi, lo = dense_of(values, rel_rows, block_slots, live_blocks)
    pieces = row_pieces(start_block, hi)
    back = swap(backward(hi, lo, pieces, needs_out))
    sums = row_sums(*forward(True, need, hi, lo, cols))
    y, pay, needs, slices = first_image(start_block, deg, sums, back)

    cols = swap(pay)
    pieces, part = row_pieces_and_sums(y, slices, z, core)
    back = backward(hi, lo, pieces, part)
    cols, back = lax.optimization_barrier((cols, back))
    back = swap(back)
    sums = row_sums(*forward(False, need, hi, lo, cols))
    back, *sums = lax.optimization_barrier((back, *sums))
    part = back[:, 128:, :].sum(0)
    near = jnp.concatenate([part, *(lax.ppermute(part, "row", along_z(k)) for k in (1, 2, 3))])
    far = lax.ppermute(near, "row", CORE)
    y2 = image(y, deg, sums, back, needs)
    alpha, beta, v0, v1, w, gram = second_block(jnp.stack([z, core]), start_block, y, y2, near, far)
    return tuple(last_block(v0, v1, w, sum_all(gram), alpha, beta))


def solution(mesh):
    return jax.shard_map(
        on_device,
        mesh=mesh,
        in_specs=(
            P(("row", "col"), None),
            P(("row", "col")),
            P(("row", "col"), None),
            P(("row", "col")),
            P(("row", "col")),
            P(("row", "col"), None),
            P(("row", "col")),
        ),
        out_specs=(P(), P(), P(("row", "col"), None)),
        check_vma=False,
    )
```

```python
import functools

import jax
import jax.numpy as jnp
from jax import lax
from jax.experimental import pallas as pl
from jax.experimental.pallas import tpu as pltpu
from jax.sharding import PartitionSpec as P

BS = 64
RB = 4
KS = 2
NB = 128
ROWS = RB * BS
N_ROW = 8
N_COL = 16
NROWS = ROWS * N_ROW * N_COL
CAP = 384
SIDE = 2048
SHIFT = 4.0
GROUPS = CAP // 8
STEP_GROUPS = 6
FILL_STEPS = GROUPS // STEP_GROUPS
CHUNK = 256
CHUNKS = SIDE // CHUNK
PART = NB // N_ROW
SLICE = 3 * PART

HIGH = lax.Precision.HIGHEST
F32, BF16 = jnp.float32, jnp.bfloat16
MIB = 2**20


def mm(a, b, ca=1, cb=0):
    return lax.dot_general(a, b, (((ca,), (cb,)), ((), ())), precision=HIGH, preferred_element_type=F32)


def split(x):
    high = x.astype(BF16)
    return high, (x - high.astype(F32)).astype(BF16)


def dense_kernel(rows_ref, slots_ref, live_ref, vals_ref, hi_ref, lo_ref, dense):
    i = pl.program_id(0)
    live = live_ref[0]

    @pl.when(i == 0)
    def _():
        def clear(t, c):
            dense[t // 8, pl.ds(pl.multiple_of((t % 8) * 256, 256), 256), :] = jnp.zeros((256, 128), F32)
            return c

        lax.fori_loop(0, 128, clear, 0)

    half = lax.broadcasted_iota(jnp.int32, (32, 128), 1) // 64

    @pl.when(i < FILL_STEPS)
    def _():
        def group(g, c):
            for s in range(8):
                slot = (i * STEP_GROUPS + g) * 8 + s
                first = rows_ref[slot] * BS
                q = slots_ref[slot]
                side = jnp.where(slot < live, q % 2, 2)
                two = vals_ref[g, pl.ds(s, 32, stride=8), :]
                turned = pltpu.roll(two, 64, 1)
                even = jnp.where(half == side, jnp.where(half == 0, two, turned), 0.0)
                odd = jnp.where(half == side, jnp.where(half == 0, turned, two), 0.0)
                dense[q // 2, pl.ds(first, 32, stride=2), :] += even
                dense[q // 2, pl.ds(first + 1, 32, stride=2), :] += odd
            return c

        left = (live + 7) // 8 - i * STEP_GROUPS
        lax.fori_loop(0, jnp.clip(left, 0, STEP_GROUPS), group, 0)

    @pl.when(i >= FILL_STEPS)
    def _():
        first = pl.multiple_of((i - FILL_STEPS) * CHUNK, CHUNK)
        for j in range(16):
            high, low = split(dense[j, pl.ds(first, CHUNK), :])
            hi_ref[:, j * 128 : (j + 1) * 128] = high
            lo_ref[:, j * 128 : (j + 1) * 128] = low


def dense_of(values, rel_rows, slots, live):
    grid = FILL_STEPS + CHUNKS
    out = pl.BlockSpec((CHUNK, SIDE), lambda i, *_: (jnp.maximum(i - FILL_STEPS, 0), 0))
    return pl.pallas_call(
        dense_kernel,
        grid_spec=pltpu.PrefetchScalarGridSpec(
            num_scalar_prefetch=3,
            grid=(grid,),
            in_specs=[pl.BlockSpec((STEP_GROUPS, 256, 128), lambda i, *_: (jnp.minimum(i, FILL_STEPS - 1), 0, 0))],
            out_specs=[out, out],
            scratch_shapes=[pltpu.VMEM((16, SIDE, 128), F32)],
        ),
        out_shape=[jax.ShapeDtypeStruct((SIDE, SIDE), BF16)] * 2,
        compiler_params=pltpu.CompilerParams(vmem_limit_bytes=56 * MIB),
        cost_estimate=pl.CostEstimate(flops=10**7, bytes_accessed=50 * 10**6, transcendentals=0),
        name="dense",
    )(rel_rows, slots, live, values)


def fetches(columns, i, hi_any, lo_any, hi, lo, sems):
    here = pl.ds(pl.multiple_of(i * CHUNK, CHUNK), CHUNK)
    at = (slice(None), here) if columns else (here, slice(None))
    return [
        pltpu.make_async_copy(src.at[at], dst.at[at], sems.at[n, i])
        for n, (src, dst) in enumerate(((hi_any, hi), (lo_any, lo)))
    ]


def begin_fetches(columns, *refs):
    def begin(i, c):
        for copy in fetches(columns, i, *refs):
            copy.start()
        return c

    lax.fori_loop(0, CHUNKS, begin, 0)


def forward_kernel(whole, need_ref, hi_any, lo_any, cols, keep, send, hi, lo, xc, sems):
    begin_fetches(False, hi_any, lo_any, hi, lo, sems)

    def column(p, c):
        for k in range(KS):
            if whole:
                first = jnp.minimum(need_ref[p * KS + k], RB - 1) * BS
                block = cols[p, pl.ds(pl.multiple_of(first, BS), BS), :]
            else:
                block = cols[p, k * BS : (k + 1) * BS, :]
            high, low = split(block)
            here = pl.ds(pl.multiple_of((p * KS + k) * BS, BS), BS)
            xc[here, 0:128] = high
            xc[here, 128:256] = low
        return c

    lax.fori_loop(0, N_COL, column, 0)

    def chunk(i, c):
        here = pl.ds(pl.multiple_of(i * CHUNK, CHUNK), CHUNK)
        x = xc[...]
        for copy in fetches(False, i, hi_any, lo_any, hi, lo, sems):
            copy.wait()
        out = jnp.dot(hi[here, :], x, preferred_element_type=F32) + jnp.dot(lo[here, :], x, preferred_element_type=F32)
        out = out[:, :128] + out[:, 128:]

        @pl.when(i < 4)
        def _():
            keep[jnp.minimum(i, 3)] = out

        @pl.when(i >= 4)
        def _():
            send[jnp.maximum(i - 4, 0)] = out

        return c

    lax.fori_loop(0, CHUNKS, chunk, 0)


def backward_kernel(hi_any, lo_any, own, z1, z2, z3, far, extra, pay, hi, lo, xr, sems):
    begin_fetches(True, hi_any, lo_any, hi, lo, sems)
    for c in range(CHUNKS):
        piece = (own, z1, z2, z3)[c][0:ROWS, :] if c < 4 else far[(c - 4) * CHUNK : (c - 3) * CHUNK, :]
        high, low = split(piece.T)
        xr[0:128, c * CHUNK : (c + 1) * CHUNK] = high
        xr[128:256, c * CHUNK : (c + 1) * CHUNK] = low

    def chunk(j, c):
        here = pl.ds(pl.multiple_of(j * CHUNK, CHUNK), CHUNK)
        v = xr[...]
        for copy in fetches(True, j, hi_any, lo_any, hi, lo, sems):
            copy.wait()
        out = jnp.dot(v, hi[:, here], preferred_element_type=F32)
        out = (out[:128] + out[128:] + jnp.dot(v[:128], lo[:, here], preferred_element_type=F32)).T
        for q in range(2):
            p = j * 2 + q
            pay[p, 0:128, :] = out[q * 128 : (q + 1) * 128]
            pay[p, 128:, :] = extra[p] if len(extra.shape) == 3 else extra[...]
        return c

    lax.fori_loop(0, CHUNKS, chunk, 0)


VMEM = pl.BlockSpec(memory_space=pltpu.VMEM)
ANYWHERE = pl.BlockSpec(memory_space=pl.ANY)
PRODUCT = {
    "compiler_params": pltpu.CompilerParams(vmem_limit_bytes=50 * MIB),
    "cost_estimate": pl.CostEstimate(flops=10**6, bytes_accessed=10**5, transcendentals=0),
}


def forward(whole, need, hi, lo, cols):
    return pl.pallas_call(
        functools.partial(forward_kernel, whole),
        in_specs=[pl.BlockSpec(memory_space=pltpu.SMEM), ANYWHERE, ANYWHERE, VMEM],
        out_specs=[VMEM] * 2,
        scratch_shapes=[
            pltpu.VMEM((SIDE, SIDE), BF16),
            pltpu.VMEM((SIDE, SIDE), BF16),
            pltpu.VMEM((SIDE, 256), BF16),
            pltpu.SemaphoreType.DMA((2, CHUNKS)),
        ],
        out_shape=[jax.ShapeDtypeStruct((4, ROWS, NB), F32)] * 2,
        name="forward",
        **PRODUCT,
    )(need, hi, lo, cols)


def backward(hi, lo, pieces, extra):
    return pl.pallas_call(
        backward_kernel,
        in_specs=[ANYWHERE, ANYWHERE] + [VMEM] * 6,
        out_specs=VMEM,
        scratch_shapes=[
            pltpu.VMEM((SIDE, SIDE), BF16),
            pltpu.VMEM((SIDE, SIDE), BF16),
            pltpu.VMEM((256, SIDE), BF16),
            pltpu.SemaphoreType.DMA((2, CHUNKS)),
        ],
        out_shape=jax.ShapeDtypeStruct((N_COL, 128 + extra.shape[-2], NB), F32),
        name="backward",
        **PRODUCT,
    )(hi, lo, *pieces, extra)


def image_of(v, deg, s0, s1, s2, s3, arrived, needs):
    sums = s0[...] + s1[...] + s2[...] + s3[...]

    def peer(p, parts):
        for q in range(KS):
            block = arrived[p, q * BS : (q + 1) * BS, :]
            which = needs[p, q : q + 1, :]
            parts = tuple(parts[k] + jnp.where(which == float(k), block, 0.0) for k in range(RB))
        return parts

    zero = jnp.zeros((BS, NB), F32)
    parts = lax.fori_loop(0, N_COL, peer, (zero,) * RB)
    return (deg[...] - SHIFT) * v[...] - sums - jnp.concatenate(parts, axis=0)


def first_kernel(v, deg, s0, s1, s2, s3, arrived, image, pay, needs, slices):
    needs[...] = arrived[:, 128:136, :]
    y = image_of(v, deg, s0, s1, s2, s3, arrived, needs)
    image[...] = y
    for p in range(N_COL):
        for q in range(KS):
            which = needs[p, q : q + 1, :]
            block = jnp.zeros((BS, NB), F32)
            for k in range(RB):
                block = jnp.where(which == float(k), image[k * BS : (k + 1) * BS, :], block)
            pay[p, q * BS : (q + 1) * BS, :] = block
    x = v[...]
    xt, yt = x.T, y.T
    for n, gram in enumerate((mm(xt, x), mm(xt, y), mm(yt, y))):
        gram = gram * (1.0 / NROWS)
        for r in range(N_ROW):
            slices[r, n * PART : (n + 1) * PART, :] = gram[r * PART : (r + 1) * PART, :]


def first_image(v, deg, sums, arrived):
    return pl.pallas_call(
        first_kernel,
        out_shape=[
            jax.ShapeDtypeStruct((ROWS, NB), F32),
            jax.ShapeDtypeStruct((N_COL, 128, NB), F32),
            jax.ShapeDtypeStruct((N_COL, 8, NB), F32),
            jax.ShapeDtypeStruct((N_ROW, SLICE, NB), F32),
        ],
        compiler_params=pltpu.CompilerParams(vmem_limit_bytes=32 * MIB),
        name="first_image",
    )(v, deg, *sums, arrived)


PANEL = 64
WINDOW = 8


def factor(a):
    z = eye()
    row = lax.broadcasted_iota(jnp.int32, (PANEL, NB), 0)
    uppers, inverses = [], []
    for b in range(NB // PANEL):
        pa, pz = a[:PANEL], z[:PANEL]
        da = dz = jnp.zeros((PANEL, NB), F32)
        for t in range(0, PANEL, WINDOW):
            k = b * PANEL + t
            here = range(WINDOW)
            cols = [jnp.broadcast_to(pa[:, k + i : k + i + 1], (PANEL, NB)) for i in here]
            ra = [pa[t + i : t + i + 1, :] for i in here]
            rz = [pz[t + i : t + i + 1, :] for i in here]
            tops = [[cols[j][t + i : t + i + 1, :] for j in here] for i in here]
            for i in here:
                root = lax.rsqrt(tops[i][i])
                inverse = root * root
                for j in range(i + 1, WINDOW):
                    times = tops[i][j] * inverse
                    ra[j] = ra[j] - times * ra[i]
                    rz[j] = rz[j] - times * rz[i]
                    cols[j] = cols[j] - times * cols[i]
                    for m in range(j, WINDOW):
                        tops[j][m] = tops[j][m] - times * tops[i][m]
                da = jnp.where(row == t + i, ra[i] * root, da)
                dz = jnp.where(row == t + i, rz[i] * root, dz)
                cols[i] = cols[i] * inverse
            for i in here:
                pa = pa - cols[i] * ra[i]
                pz = pz - cols[i] * rz[i]
        uppers.append(da)
        inverses.append(dz)
        if b < NB // PANEL - 1:
            left = da.T[(b + 1) * PANEL :, :]
            a = a[PANEL:] - mm(left, da)
            z = z[PANEL:] - mm(left, dz)
    lane = lax.broadcasted_iota(jnp.int32, (NB, NB), 1)
    sub = lax.broadcasted_iota(jnp.int32, (NB, NB), 0)
    return jnp.where(lane >= sub, jnp.concatenate(uppers, axis=0), 0.0), jnp.concatenate(inverses, axis=0)


def eye():
    return jnp.where(
        lax.broadcasted_iota(jnp.int32, (NB, NB), 0) == lax.broadcasted_iota(jnp.int32, (NB, NB), 1), 1.0, 0.0
    )


def image_kernel(v, deg, s0, s1, s2, s3, arrived, needs, image):
    image[...] = image_of(v, deg, s0, s1, s2, s3, arrived, needs)


def image(v, deg, sums, arrived, needs):
    return pl.pallas_call(
        image_kernel,
        out_shape=jax.ShapeDtypeStruct((ROWS, NB), F32),
        compiler_params=pltpu.CompilerParams(vmem_limit_bytes=32 * MIB),
        name="image",
    )(v, deg, *sums, arrived, needs)


def second_kernel(place, x_ref, y_ref, y2_ref, near, far, alpha, beta, v0_ref, v1_ref, w_ref, gram, grams):
    z, core = place[0], place[1]
    for k in range(4):
        here = slice(k * SLICE, (k + 1) * SLICE)
        grams[(z ^ k) * 2 + core] = near[here, :]
        grams[(z ^ k) * 2 + (1 - core)] = far[here, :]
    y2 = y2_ref[...]
    xx, xy, yy = (
        jnp.concatenate([grams[r, n * PART : (n + 1) * PART, :] for r in range(N_ROW)], axis=0) for n in range(3)
    )
    x, y = x_ref[...], y_ref[...]
    _, inv0 = factor(xx)
    a0 = mm(mm(inv0, xy), inv0, 1, 1)
    b0 = mm(mm(inv0, yy), inv0, 1, 1)
    alpha[...] = a0 + SHIFT * eye()
    upper1, inv1 = factor(b0 - mm(a0, a0, 0, 0))
    beta[...] = upper1
    v0 = mm(x, inv0, 1, 1)
    t = mm(inv0, inv1, 0, 1)
    u = mm(mm(inv0, a0, 0, 0), inv1, 1, 1)
    v1 = mm(y, t) - mm(x, u)
    w = mm(y2, t) - mm(y, u)
    v0_ref[...], v1_ref[...], w_ref[...] = v0, v1, w
    gram[0:128, :] = mm(v0.T, w) * (1.0 / NROWS)
    gram[128:256, :] = mm(v1.T, w) * (1.0 / NROWS)
    gram[256:384, :] = mm(w.T, w) * (1.0 / NROWS)


def second_block(*args):
    square = jax.ShapeDtypeStruct((NB, NB), F32)
    owned = jax.ShapeDtypeStruct((ROWS, NB), F32)
    return pl.pallas_call(
        second_kernel,
        in_specs=[pl.BlockSpec(memory_space=pltpu.SMEM)] + [VMEM] * 5,
        out_specs=[VMEM] * 6,
        out_shape=[square, square, owned, owned, owned, jax.ShapeDtypeStruct((3 * NB, NB), F32)],
        scratch_shapes=[pltpu.VMEM((N_ROW, SLICE, NB), F32)],
        compiler_params=pltpu.CompilerParams(vmem_limit_bytes=32 * MIB),
        name="second_block",
    )(*args)


def last_kernel(v0, v1, w, gram, alpha0, beta0, alphas, betas, basis):
    a0, a1, b = gram[0:128, :], gram[128:256, :], gram[256:384, :]
    upper, inv = factor(b - mm(a0, a0, 0, 0) - mm(a1, a1, 0, 0))
    alphas[0], betas[0] = alpha0[...], beta0[...]
    alphas[1] = a1 + SHIFT * eye()
    betas[1] = upper
    w2 = w[...] - mm(v0[...], a0) - mm(v1[...], a1)
    basis[...] = mm(w2, inv, 1, 1)


def last_block(*args):
    pair = jax.ShapeDtypeStruct((2, NB, NB), F32)
    return pl.pallas_call(
        last_kernel,
        out_shape=[pair, pair, jax.ShapeDtypeStruct((ROWS, NB), F32)],
        compiler_params=pltpu.CompilerParams(vmem_limit_bytes=32 * MIB),
        name="last_block",
    )(*args)


CORE = [(i, i ^ 1) for i in range(N_ROW)]


def along_z(k):
    return [(i, ((i // 2) ^ k) * 2 + i % 2) for i in range(N_ROW)]


def along_x(k):
    return [(i, ((i // 4) ^ k) * 4 + i % 4) for i in range(N_COL)]


def along_y(k):
    return [(i, (i // 4) * 4 + ((i % 4) ^ k)) for i in range(N_COL)]


def row_pieces(own, *after):
    three = [lax.ppermute(own, "row", along_z(k)) for k in (1, 2, 3)]
    if after:
        *three, _ = lax.optimization_barrier((*three, *after))
    far = lax.ppermute(jnp.concatenate([own, *three]), "row", CORE)
    return [own, *three, far]


def row_pieces_and_sums(own, slices, z, core):
    chips = slices.reshape(N_ROW // 2, 2 * SLICE, NB)
    three = [lax.ppermute(jnp.concatenate([own, chips[z ^ k]]), "row", along_z(k)) for k in (1, 2, 3)]
    a, b, c = (got[ROWS:] for got in three)
    pair = ((chips[z] + a) + (b + c)).reshape(2, SLICE, NB)
    far = lax.ppermute(jnp.concatenate([own, *(got[:ROWS] for got in three), pair[1 - core]]), "row", CORE)
    return [own, *three, far], pair[core] + far[4 * ROWS :]


def row_sums(keep, send):
    other = lax.ppermute(send, "row", CORE)
    parts = [keep[k] + other[k] for k in range(4)]
    return [parts[0]] + [lax.ppermute(parts[k], "row", along_z(k)) for k in (1, 2, 3)]


def swap(x):
    return lax.all_to_all(x, "col", 0, 0)


def ring_sum(x, axis, shift):
    a, b, c = (lax.ppermute(x, axis, shift(k)) for k in (1, 2, 3))
    return (x + a) + (b + c)


def sum_all(x):
    core = lax.axis_index("row") % 2
    n = x.shape[0] // 2
    here = jnp.where(core == 0, x[:n], x[n:])
    there = jnp.where(core == 0, x[n:], x[:n])
    here = here + lax.ppermute(there, "row", CORE)
    here = ring_sum(here, "row", along_z)
    here = ring_sum(here, "col", along_x)
    here = ring_sum(here, "col", along_y)
    other = lax.ppermute(here, "row", CORE)
    return jnp.concatenate([jnp.where(core == 0, here, other), jnp.where(core == 0, other, here)])


def on_device(start_block, degree, block_values, block_rows, block_slots, need_lists, live_blocks):
    row = lax.axis_index("row")
    z, core = row // 2, row % 2
    owner, k = block_rows // RB, block_rows % RB
    rel_rows = (((owner % 2) ^ core) * 4 + ((owner // 2) ^ z)) * RB + k
    need = need_lists.reshape(-1)
    needs_out = jnp.broadcast_to(
        jnp.pad(need_lists.astype(F32), ((0, 0), (0, 8 - KS)))[:, :, None], (N_COL, 8, NB)
    )
    deg = jnp.broadcast_to(degree[:, None], (ROWS, NB))
    values = block_values.reshape(GROUPS, 8, 32, 128).transpose(0, 2, 1, 3).reshape(GROUPS, 256, 128)

    cols = swap(jnp.broadcast_to(start_block[None], (N_COL, ROWS, NB)))
    hi, lo = dense_of(values, rel_rows, block_slots, live_blocks)
    pieces = row_pieces(start_block, hi)
    back = swap(backward(hi, lo, pieces, needs_out))
    sums = row_sums(*forward(True, need, hi, lo, cols))
    y, pay, needs, slices = first_image(start_block, deg, sums, back)

    cols = swap(pay)
    pieces, part = row_pieces_and_sums(y, slices, z, core)
    back = backward(hi, lo, pieces, part)
    cols, back = lax.optimization_barrier((cols, back))
    back = swap(back)
    sums = row_sums(*forward(False, need, hi, lo, cols))
    back, *sums = lax.optimization_barrier((back, *sums))
    part = back[:, 128:, :].sum(0)
    near = jnp.concatenate([part, *(lax.ppermute(part, "row", along_z(k)) for k in (1, 2, 3))])
    far = lax.ppermute(near, "row", CORE)
    y2 = image(y, deg, sums, back, needs)
    alpha, beta, v0, v1, w, gram = second_block(jnp.stack([z, core]), start_block, y, y2, near, far)
    return tuple(last_block(v0, v1, w, sum_all(gram), alpha, beta))


def solution(mesh):
    return jax.shard_map(
        on_device,
        mesh=mesh,
        in_specs=(
            P(("row", "col"), None),
            P(("row", "col")),
            P(("row", "col"), None),
            P(("row", "col")),
            P(("row", "col")),
            P(("row", "col"), None),
            P(("row", "col")),
        ),
        out_specs=(P(), P(), P(("row", "col"), None)),
        check_vma=False,
    )
```

```python
import functools

import jax
import jax.numpy as jnp
from jax import lax
from jax.experimental import pallas as pl
from jax.experimental.pallas import tpu as pltpu
from jax.sharding import PartitionSpec as P

BS = 64
RB = 4
KS = 2
NB = 128
ROWS = RB * BS
N_ROW = 8
N_COL = 16
NROWS = ROWS * N_ROW * N_COL
CAP = 384
SIDE = 2048
SHIFT = 4.0
GROUPS = CAP // 8
STEP_GROUPS = 6
FILL_STEPS = GROUPS // STEP_GROUPS
CHUNK = 256
CHUNKS = SIDE // CHUNK
PART = NB // N_ROW
SLICE = 3 * PART

HIGH = lax.Precision.HIGHEST
F32, BF16 = jnp.float32, jnp.bfloat16
MIB = 2**20


def mm(a, b, ca=1, cb=0):
    return lax.dot_general(a, b, (((ca,), (cb,)), ((), ())), precision=HIGH, preferred_element_type=F32)


def split(x):
    high = x.astype(BF16)
    return high, (x - high.astype(F32)).astype(BF16)


def dense_kernel(rows_ref, slots_ref, live_ref, vals_ref, hi_ref, lo_ref, dense):
    i = pl.program_id(0)
    live = live_ref[0]

    @pl.when(i == 0)
    def _():
        def clear(t, c):
            dense[t // 8, pl.ds(pl.multiple_of((t % 8) * 256, 256), 256), :] = jnp.zeros((256, 128), F32)
            return c

        lax.fori_loop(0, 128, clear, 0)

    half = lax.broadcasted_iota(jnp.int32, (32, 128), 1) // 64

    @pl.when(i < FILL_STEPS)
    def _():
        def group(g, c):
            for s in range(8):
                slot = (i * STEP_GROUPS + g) * 8 + s
                first = rows_ref[slot] * BS
                q = slots_ref[slot]
                side = jnp.where(slot < live, q % 2, 2)
                two = vals_ref[g, pl.ds(s, 32, stride=8), :]
                turned = pltpu.roll(two, 64, 1)
                even = jnp.where(half == side, jnp.where(half == 0, two, turned), 0.0)
                odd = jnp.where(half == side, jnp.where(half == 0, turned, two), 0.0)
                dense[q // 2, pl.ds(first, 32, stride=2), :] += even
                dense[q // 2, pl.ds(first + 1, 32, stride=2), :] += odd
            return c

        left = (live + 7) // 8 - i * STEP_GROUPS
        lax.fori_loop(0, jnp.clip(left, 0, STEP_GROUPS), group, 0)

    @pl.when(i >= FILL_STEPS)
    def _():
        first = pl.multiple_of((i - FILL_STEPS) * CHUNK, CHUNK)
        for j in range(16):
            high, low = split(dense[j, pl.ds(first, CHUNK), :])
            hi_ref[:, j * 128 : (j + 1) * 128] = high
            lo_ref[:, j * 128 : (j + 1) * 128] = low


def dense_of(values, rel_rows, slots, live):
    grid = FILL_STEPS + CHUNKS
    out = pl.BlockSpec((CHUNK, SIDE), lambda i, *_: (jnp.maximum(i - FILL_STEPS, 0), 0))
    return pl.pallas_call(
        dense_kernel,
        grid_spec=pltpu.PrefetchScalarGridSpec(
            num_scalar_prefetch=3,
            grid=(grid,),
            in_specs=[pl.BlockSpec((STEP_GROUPS, 256, 128), lambda i, *_: (jnp.minimum(i, FILL_STEPS - 1), 0, 0))],
            out_specs=[out, out],
            scratch_shapes=[pltpu.VMEM((16, SIDE, 128), F32)],
        ),
        out_shape=[jax.ShapeDtypeStruct((SIDE, SIDE), BF16)] * 2,
        compiler_params=pltpu.CompilerParams(vmem_limit_bytes=56 * MIB),
        cost_estimate=pl.CostEstimate(flops=10**7, bytes_accessed=50 * 10**6, transcendentals=0),
        name="dense",
    )(rel_rows, slots, live, values)


def fetches(columns, i, hi_any, lo_any, hi, lo, sems):
    here = pl.ds(pl.multiple_of(i * CHUNK, CHUNK), CHUNK)
    at = (slice(None), here) if columns else (here, slice(None))
    return [
        pltpu.make_async_copy(src.at[at], dst.at[at], sems.at[n, i])
        for n, (src, dst) in enumerate(((hi_any, hi), (lo_any, lo)))
    ]


def begin_fetches(columns, *refs):
    def begin(i, c):
        for copy in fetches(columns, i, *refs):
            copy.start()
        return c

    lax.fori_loop(0, CHUNKS, begin, 0)


def forward_kernel(whole, need_ref, hi_any, lo_any, cols, keep, send, hi, lo, xc, sems):
    begin_fetches(False, hi_any, lo_any, hi, lo, sems)

    def column(p, c):
        for k in range(KS):
            if whole:
                first = jnp.minimum(need_ref[p * KS + k], RB - 1) * BS
                block = cols[p, pl.ds(pl.multiple_of(first, BS), BS), :]
            else:
                block = cols[p, k * BS : (k + 1) * BS, :]
            high, low = split(block)
            here = pl.ds(pl.multiple_of((p * KS + k) * BS, BS), BS)
            xc[here, 0:128] = high
            xc[here, 128:256] = low
        return c

    lax.fori_loop(0, N_COL, column, 0)

    def chunk(i, c):
        here = pl.ds(pl.multiple_of(i * CHUNK, CHUNK), CHUNK)
        x = xc[...]
        for copy in fetches(False, i, hi_any, lo_any, hi, lo, sems):
            copy.wait()
        out = jnp.dot(hi[here, :], x, preferred_element_type=F32)
        out = out[:, :128] + out[:, 128:] + jnp.dot(lo[here, :], x[:, :128], preferred_element_type=F32)

        @pl.when(i < 4)
        def _():
            keep[jnp.minimum(i, 3)] = out

        @pl.when(i >= 4)
        def _():
            send[jnp.maximum(i - 4, 0)] = out

        return c

    lax.fori_loop(0, CHUNKS, chunk, 0)


def backward_kernel(hi_any, lo_any, own, z1, z2, z3, far, extra, pay, hi, lo, xr, sems):
    begin_fetches(True, hi_any, lo_any, hi, lo, sems)
    for c in range(CHUNKS):
        piece = (own, z1, z2, z3)[c][0:ROWS, :] if c < 4 else far[(c - 4) * CHUNK : (c - 3) * CHUNK, :]
        high, low = split(piece.T)
        xr[0:128, c * CHUNK : (c + 1) * CHUNK] = high
        xr[128:256, c * CHUNK : (c + 1) * CHUNK] = low

    def chunk(j, c):
        here = pl.ds(pl.multiple_of(j * CHUNK, CHUNK), CHUNK)
        v = xr[...]
        for copy in fetches(True, j, hi_any, lo_any, hi, lo, sems):
            copy.wait()
        out = jnp.dot(v, hi[:, here], preferred_element_type=F32)
        out = (out[:128] + out[128:] + jnp.dot(v[:128], lo[:, here], preferred_element_type=F32)).T
        for q in range(2):
            p = j * 2 + q
            pay[p, 0:128, :] = out[q * 128 : (q + 1) * 128]
            pay[p, 128:, :] = extra[p] if len(extra.shape) == 3 else extra[...]
        return c

    lax.fori_loop(0, CHUNKS, chunk, 0)


VMEM = pl.BlockSpec(memory_space=pltpu.VMEM)
ANYWHERE = pl.BlockSpec(memory_space=pl.ANY)
PRODUCT = {
    "compiler_params": pltpu.CompilerParams(vmem_limit_bytes=50 * MIB),
    "cost_estimate": pl.CostEstimate(flops=10**6, bytes_accessed=10**5, transcendentals=0),
}


def forward(whole, need, hi, lo, cols):
    return pl.pallas_call(
        functools.partial(forward_kernel, whole),
        in_specs=[pl.BlockSpec(memory_space=pltpu.SMEM), ANYWHERE, ANYWHERE, VMEM],
        out_specs=[VMEM] * 2,
        scratch_shapes=[
            pltpu.VMEM((SIDE, SIDE), BF16),
            pltpu.VMEM((SIDE, SIDE), BF16),
            pltpu.VMEM((SIDE, 256), BF16),
            pltpu.SemaphoreType.DMA((2, CHUNKS)),
        ],
        out_shape=[jax.ShapeDtypeStruct((4, ROWS, NB), F32)] * 2,
        name="forward",
        **PRODUCT,
    )(need, hi, lo, cols)


def backward(hi, lo, pieces, extra):
    return pl.pallas_call(
        backward_kernel,
        in_specs=[ANYWHERE, ANYWHERE] + [VMEM] * 6,
        out_specs=VMEM,
        scratch_shapes=[
            pltpu.VMEM((SIDE, SIDE), BF16),
            pltpu.VMEM((SIDE, SIDE), BF16),
            pltpu.VMEM((256, SIDE), BF16),
            pltpu.SemaphoreType.DMA((2, CHUNKS)),
        ],
        out_shape=jax.ShapeDtypeStruct((N_COL, 128 + extra.shape[-2], NB), F32),
        name="backward",
        **PRODUCT,
    )(hi, lo, *pieces, extra)


def image_of(v, deg, s0, s1, s2, s3, arrived, needs):
    sums = s0[...] + s1[...] + s2[...] + s3[...]

    def peer(p, parts):
        for q in range(KS):
            block = arrived[p, q * BS : (q + 1) * BS, :]
            which = needs[p, q : q + 1, :]
            parts = tuple(parts[k] + jnp.where(which == float(k), block, 0.0) for k in range(RB))
        return parts

    zero = jnp.zeros((BS, NB), F32)
    parts = lax.fori_loop(0, N_COL, peer, (zero,) * RB)
    return (deg[...] - SHIFT) * v[...] - sums - jnp.concatenate(parts, axis=0)


def first_kernel(v, deg, s0, s1, s2, s3, arrived, image, pay, needs, slices):
    needs[...] = arrived[:, 128:136, :]
    y = image_of(v, deg, s0, s1, s2, s3, arrived, needs)
    image[...] = y
    for p in range(N_COL):
        for q in range(KS):
            which = needs[p, q : q + 1, :]
            block = jnp.zeros((BS, NB), F32)
            for k in range(RB):
                block = jnp.where(which == float(k), image[k * BS : (k + 1) * BS, :], block)
            pay[p, q * BS : (q + 1) * BS, :] = block
    x = v[...]
    xt, yt = x.T, y.T
    for n, gram in enumerate((mm(xt, x), mm(xt, y), mm(yt, y))):
        gram = gram * (1.0 / NROWS)
        for r in range(N_ROW):
            slices[r, n * PART : (n + 1) * PART, :] = gram[r * PART : (r + 1) * PART, :]


def first_image(v, deg, sums, arrived):
    return pl.pallas_call(
        first_kernel,
        out_shape=[
            jax.ShapeDtypeStruct((ROWS, NB), F32),
            jax.ShapeDtypeStruct((N_COL, 128, NB), F32),
            jax.ShapeDtypeStruct((N_COL, 8, NB), F32),
            jax.ShapeDtypeStruct((N_ROW, SLICE, NB), F32),
        ],
        compiler_params=pltpu.CompilerParams(vmem_limit_bytes=32 * MIB),
        name="first_image",
    )(v, deg, *sums, arrived)


PANEL = 64
WINDOW = 8


def factor(a):
    z = eye()
    row = lax.broadcasted_iota(jnp.int32, (PANEL, NB), 0)
    uppers, inverses = [], []
    for b in range(NB // PANEL):
        pa, pz = a[:PANEL], z[:PANEL]
        da = dz = jnp.zeros((PANEL, NB), F32)
        for t in range(0, PANEL, WINDOW):
            k = b * PANEL + t
            here = range(WINDOW)
            cols = [jnp.broadcast_to(pa[:, k + i : k + i + 1], (PANEL, NB)) for i in here]
            ra = [pa[t + i : t + i + 1, :] for i in here]
            rz = [pz[t + i : t + i + 1, :] for i in here]
            tops = [[cols[j][t + i : t + i + 1, :] for j in here] for i in here]
            for i in here:
                root = lax.rsqrt(tops[i][i])
                inverse = root * root
                for j in range(i + 1, WINDOW):
                    times = tops[i][j] * inverse
                    ra[j] = ra[j] - times * ra[i]
                    rz[j] = rz[j] - times * rz[i]
                    cols[j] = cols[j] - times * cols[i]
                    for m in range(j, WINDOW):
                        tops[j][m] = tops[j][m] - times * tops[i][m]
                da = jnp.where(row == t + i, ra[i] * root, da)
                dz = jnp.where(row == t + i, rz[i] * root, dz)
                cols[i] = cols[i] * inverse
            for i in here:
                pa = pa - cols[i] * ra[i]
                pz = pz - cols[i] * rz[i]
        uppers.append(da)
        inverses.append(dz)
        if b < NB // PANEL - 1:
            left = da.T[(b + 1) * PANEL :, :]
            a = a[PANEL:] - mm(left, da)
            z = z[PANEL:] - mm(left, dz)
    lane = lax.broadcasted_iota(jnp.int32, (NB, NB), 1)
    sub = lax.broadcasted_iota(jnp.int32, (NB, NB), 0)
    return jnp.where(lane >= sub, jnp.concatenate(uppers, axis=0), 0.0), jnp.concatenate(inverses, axis=0)


def eye():
    return jnp.where(
        lax.broadcasted_iota(jnp.int32, (NB, NB), 0) == lax.broadcasted_iota(jnp.int32, (NB, NB), 1), 1.0, 0.0
    )


def image_kernel(v, deg, s0, s1, s2, s3, arrived, needs, image):
    image[...] = image_of(v, deg, s0, s1, s2, s3, arrived, needs)


def image(v, deg, sums, arrived, needs):
    return pl.pallas_call(
        image_kernel,
        out_shape=jax.ShapeDtypeStruct((ROWS, NB), F32),
        compiler_params=pltpu.CompilerParams(vmem_limit_bytes=32 * MIB),
        name="image",
    )(v, deg, *sums, arrived, needs)


def second_kernel(place, x_ref, y_ref, y2_ref, near, far, alpha, beta, v0_ref, v1_ref, w_ref, gram, grams):
    z, core = place[0], place[1]
    for k in range(4):
        here = slice(k * SLICE, (k + 1) * SLICE)
        grams[(z ^ k) * 2 + core] = near[here, :]
        grams[(z ^ k) * 2 + (1 - core)] = far[here, :]
    y2 = y2_ref[...]
    xx, xy, yy = (
        jnp.concatenate([grams[r, n * PART : (n + 1) * PART, :] for r in range(N_ROW)], axis=0) for n in range(3)
    )
    x, y = x_ref[...], y_ref[...]
    _, inv0 = factor(xx)
    a0 = mm(mm(inv0, xy), inv0, 1, 1)
    b0 = mm(mm(inv0, yy), inv0, 1, 1)
    alpha[...] = a0 + SHIFT * eye()
    upper1, inv1 = factor(b0 - mm(a0, a0, 0, 0))
    beta[...] = upper1
    v0 = mm(x, inv0, 1, 1)
    t = mm(inv0, inv1, 0, 1)
    u = mm(mm(inv0, a0, 0, 0), inv1, 1, 1)
    v1 = mm(y, t) - mm(x, u)
    w = mm(y2, t) - mm(y, u)
    v0_ref[...], v1_ref[...], w_ref[...] = v0, v1, w
    gram[0:128, :] = mm(v0.T, w) * (1.0 / NROWS)
    gram[128:256, :] = mm(v1.T, w) * (1.0 / NROWS)
    gram[256:384, :] = mm(w.T, w) * (1.0 / NROWS)


def second_block(*args):
    square = jax.ShapeDtypeStruct((NB, NB), F32)
    owned = jax.ShapeDtypeStruct((ROWS, NB), F32)
    return pl.pallas_call(
        second_kernel,
        in_specs=[pl.BlockSpec(memory_space=pltpu.SMEM)] + [VMEM] * 5,
        out_specs=[VMEM] * 6,
        out_shape=[square, square, owned, owned, owned, jax.ShapeDtypeStruct((3 * NB, NB), F32)],
        scratch_shapes=[pltpu.VMEM((N_ROW, SLICE, NB), F32)],
        compiler_params=pltpu.CompilerParams(vmem_limit_bytes=32 * MIB),
        name="second_block",
    )(*args)


def last_kernel(v0, v1, w, gram, alpha0, beta0, alphas, betas, basis):
    a0, a1, b = gram[0:128, :], gram[128:256, :], gram[256:384, :]
    upper, inv = factor(b - mm(a0, a0, 0, 0) - mm(a1, a1, 0, 0))
    alphas[0], betas[0] = alpha0[...], beta0[...]
    alphas[1] = a1 + SHIFT * eye()
    betas[1] = upper
    w2 = w[...] - mm(v0[...], a0) - mm(v1[...], a1)
    basis[...] = mm(w2, inv, 1, 1)


def last_block(*args):
    pair = jax.ShapeDtypeStruct((2, NB, NB), F32)
    return pl.pallas_call(
        last_kernel,
        out_shape=[pair, pair, jax.ShapeDtypeStruct((ROWS, NB), F32)],
        compiler_params=pltpu.CompilerParams(vmem_limit_bytes=32 * MIB),
        name="last_block",
    )(*args)


CORE = [(i, i ^ 1) for i in range(N_ROW)]


def along_z(k):
    return [(i, ((i // 2) ^ k) * 2 + i % 2) for i in range(N_ROW)]


def along_x(k):
    return [(i, ((i // 4) ^ k) * 4 + i % 4) for i in range(N_COL)]


def along_y(k):
    return [(i, (i // 4) * 4 + ((i % 4) ^ k)) for i in range(N_COL)]


def row_pieces(own, *after):
    three = [lax.ppermute(own, "row", along_z(k)) for k in (1, 2, 3)]
    if after:
        *three, _ = lax.optimization_barrier((*three, *after))
    far = lax.ppermute(jnp.concatenate([own, *three]), "row", CORE)
    return [own, *three, far]


def row_pieces_and_sums(own, slices, z, core):
    chips = slices.reshape(N_ROW // 2, 2 * SLICE, NB)
    three = [lax.ppermute(jnp.concatenate([own, chips[z ^ k]]), "row", along_z(k)) for k in (1, 2, 3)]
    a, b, c = (got[ROWS:] for got in three)
    pair = ((chips[z] + a) + (b + c)).reshape(2, SLICE, NB)
    far = lax.ppermute(jnp.concatenate([own, *(got[:ROWS] for got in three), pair[1 - core]]), "row", CORE)
    return [own, *three, far], pair[core] + far[4 * ROWS :]


def row_sums(keep, send):
    other = lax.ppermute(send, "row", CORE)
    parts = [keep[k] + other[k] for k in range(4)]
    return [parts[0]] + [lax.ppermute(parts[k], "row", along_z(k)) for k in (1, 2, 3)]


def swap(x):
    return lax.all_to_all(x, "col", 0, 0)


def ring_sum(x, axis, shift):
    a, b, c = (lax.ppermute(x, axis, shift(k)) for k in (1, 2, 3))
    return (x + a) + (b + c)


def sum_all(x):
    core = lax.axis_index("row") % 2
    n = x.shape[0] // 2
    here = jnp.where(core == 0, x[:n], x[n:])
    there = jnp.where(core == 0, x[n:], x[:n])
    here = here + lax.ppermute(there, "row", CORE)
    here = ring_sum(here, "row", along_z)
    here = ring_sum(here, "col", along_x)
    here = ring_sum(here, "col", along_y)
    other = lax.ppermute(here, "row", CORE)
    return jnp.concatenate([jnp.where(core == 0, here, other), jnp.where(core == 0, other, here)])


def on_device(start_block, degree, block_values, block_rows, block_slots, need_lists, live_blocks):
    row = lax.axis_index("row")
    z, core = row // 2, row % 2
    owner, k = block_rows // RB, block_rows % RB
    rel_rows = (((owner % 2) ^ core) * 4 + ((owner // 2) ^ z)) * RB + k
    need = need_lists.reshape(-1)
    needs_out = jnp.broadcast_to(
        jnp.pad(need_lists.astype(F32), ((0, 0), (0, 8 - KS)))[:, :, None], (N_COL, 8, NB)
    )
    deg = jnp.broadcast_to(degree[:, None], (ROWS, NB))
    values = block_values.reshape(GROUPS, 8, 32, 128).transpose(0, 2, 1, 3).reshape(GROUPS, 256, 128)

    cols = swap(jnp.broadcast_to(start_block[None], (N_COL, ROWS, NB)))
    hi, lo = dense_of(values, rel_rows, block_slots, live_blocks)
    pieces = row_pieces(start_block, hi)
    back = swap(backward(hi, lo, pieces, needs_out))
    sums = row_sums(*forward(True, need, hi, lo, cols))
    y, pay, needs, slices = first_image(start_block, deg, sums, back)

    cols = swap(pay)
    pieces, part = row_pieces_and_sums(y, slices, z, core)
    back = backward(hi, lo, pieces, part)
    cols, back = lax.optimization_barrier((cols, back))
    back = swap(back)
    sums = row_sums(*forward(False, need, hi, lo, cols))
    back, *sums = lax.optimization_barrier((back, *sums))
    part = back[:, 128:, :].sum(0)
    near = jnp.concatenate([part, *(lax.ppermute(part, "row", along_z(k)) for k in (1, 2, 3))])
    far = lax.ppermute(near, "row", CORE)
    y2 = image(y, deg, sums, back, needs)
    alpha, beta, v0, v1, w, gram = second_block(jnp.stack([z, core]), start_block, y, y2, near, far)
    return tuple(last_block(v0, v1, w, sum_all(gram), alpha, beta))


def solution(mesh):
    return jax.shard_map(
        on_device,
        mesh=mesh,
        in_specs=(
            P(("row", "col"), None),
            P(("row", "col")),
            P(("row", "col"), None),
            P(("row", "col")),
            P(("row", "col")),
            P(("row", "col"), None),
            P(("row", "col")),
        ),
        out_specs=(P(), P(), P(("row", "col"), None)),
        check_vma=False,
    )
```
